128 devices in a mesh: track: 16 (over x, z_lo, core), cross: 8 (over z_hi, y).
Axes of the slice: x: 4, y: 4, z: 4 (z_hi: 2, z_lo: 2; z = z_hi * 2 + z_lo), core: 2. Of those that a mesh axis runs over, the one named last changes fastest.
Arguments:
- order_parameter_field: float32 [8, 512, 256, 128], P(None, 'track', 'cross'), may hold values from 0 to 1
- reduced_warmth_ratio: float32 [128, 512, 256], P(('track', 'cross')), may hold values from 0.6 to 1.4
- entry_crystal_label: int32 [16, 8, 4, 8], P('track', 'cross'), may hold values from 0 to 8191, as said below
- number_of_live_entries: int32 [16, 8, 4], P('track', 'cross'), may hold values from 3 to 8
- boundary_speed_factor: float32 [8192], replicated, may hold values from 0.5 to 2
- heat_sheet_locator: int32 [128], replicated, may hold values from 0 to 127, each once
Outputs:
- new_phases: float32 [8, 512, 256, 128], P(None, 'track', 'cross')
The draws below stay inside these ranges and needn't reach their ends.
Inputs may be any that keep to these rules, and one draw needn't show every extreme that they name: `entry_crystal_label`: within a block the 8 ids are distinct.
All inputs are finite; a program needn't handle non-finite values.
Results may differ from the reference program's by a relative error of at most 0.0001.
Values sent between devices are 32-bit elements; how exact they have to be, the bound alone decides.
A program may use at most 256 MiB of HBM per device.

```python
import math
import jax
import jax.numpy as jnp
from jax import lax

GRAINS = 8192
SLOTS = 8
BLK = 32
ZBLOCKS = 4
STEPS = 2
XBLOCKS = 16
YBLOCKS = 8
SCAN_POINTS = 512
LATERAL_POINTS = 256
VERTICAL_POINTS = 128
HEAT_SHEET_ROWS = 1
DEVICES = 128


def draw_entry_crystal_label(key, part):
    key = jax.random.fold_in(key, 11)
    key_start, key_order = jax.random.split(key)
    along_x = jnp.arange(XBLOCKS, dtype=jnp.int32)[:, None, None]
    along_y = jnp.arange(YBLOCKS, dtype=jnp.int32)[None, :, None]
    along_z = jnp.arange(ZBLOCKS, dtype=jnp.int32)[None, None, :]
    jitter = jax.random.randint(key_start, (XBLOCKS, YBLOCKS, ZBLOCKS), 0, 3, dtype=jnp.int32)
    start = 2 * along_x + 3 * along_y + along_z + jitter
    start = start.at[0, 0, 0].set(0)
    start = start.at[-1, -1, -1].set(GRAINS - SLOTS)
    scores = jax.random.randint(key_order, (XBLOCKS, YBLOCKS, ZBLOCKS, SLOTS), 0, 65536, dtype=jnp.int32) * SLOTS + jnp.arange(SLOTS, dtype=jnp.int32)
    shuffled = jnp.argsort(scores, axis=-1).astype(jnp.int32)
    return (start[..., None] + shuffled) % GRAINS


def draw_number_of_live_entries(key, part):
    key = jax.random.fold_in(key, 23)
    counts = jax.random.randint(key, (XBLOCKS, YBLOCKS, ZBLOCKS), 3, SLOTS + 1, dtype=jnp.int32)
    counts = counts.at[0, 0, 0].set(SLOTS)
    return counts.at[-1, -1, -1].set(3)


def block_levels(rng, extent, shards, smallest, high):
    factor_of, own = 1.0, jax.random.fold_in(rng, 6)
    for position, shards_of in shards:
        steps = jnp.exp(jax.random.uniform(jax.random.fold_in(own, position), (shards_of,), jnp.float32, smallest / len(shards), high / len(shards)))
        factor_of = factor_of * jnp.repeat(steps, extent[position] // shards_of).reshape([-1 if axis == position else 1 for axis in range(len(extent))])
    return factor_of


def setup_inputs(seed: int = 0) -> dict:
    seeds = jax.random.split(jax.random.key(seed), 7)
    order_parameter_field = jnp.clip(1.0 * jax.random.uniform(seeds[0], (SLOTS, SCAN_POINTS, LATERAL_POINTS, VERTICAL_POINTS), jnp.float32) ** block_levels(seeds[0], (SLOTS, SCAN_POINTS, LATERAL_POINTS, VERTICAL_POINTS), ((1, 16), (2, 8)), -0.2, 0.2), 0.0, 1.0)
    reduced_warmth_ratio = jnp.clip(0.6 + 0.79999995 * jax.random.uniform(seeds[1], (VERTICAL_POINTS, SCAN_POINTS, LATERAL_POINTS), jnp.float32) ** block_levels(seeds[1], (VERTICAL_POINTS, SCAN_POINTS, LATERAL_POINTS), ((0, 128),), -0.2, 0.2), 0.6, 1.4)
    entry_crystal_label = draw_entry_crystal_label(jax.random.fold_in(seeds[6], 71), 0)
    number_of_live_entries = draw_number_of_live_entries(jax.random.fold_in(seeds[6], 71), 0)
    boundary_speed_factor = jnp.clip(jnp.exp(jax.random.uniform(seeds[4], (GRAINS,), jnp.float32, math.log(0.5), math.log(2.0))), 0.5, 2.0)
    heat_sheet_locator = jax.random.permutation(seeds[5], DEVICES).astype(jnp.int32)
    return dict(order_parameter_field=order_parameter_field, reduced_warmth_ratio=reduced_warmth_ratio, entry_crystal_label=entry_crystal_label, number_of_live_entries=number_of_live_entries, boundary_speed_factor=boundary_speed_factor, heat_sheet_locator=heat_sheet_locator)


mixing = 1.5
gradient_coef = 1.0
undercool_gain = 4.0
time_step = 0.06


def match_table(own_codes, peer_codes):
    equal_ids = (own_codes[..., :, None] == peer_codes[..., None, :]) & (own_codes[..., :, None] > 0)
    return equal_ids.astype(jnp.float32)


def remap_face(remap, face):
    slot_count, extent_w, extent_z = face.shape
    blocks = remap.shape[0]
    divided = face.reshape(slot_count, extent_w, blocks, extent_z // blocks)
    carried = jnp.einsum("kst,tykz->sykz", remap, divided, precision=lax.Precision.HIGHEST)
    return carried.reshape(slot_count, extent_w, extent_z)


def advance(field_now, heat_field, mobility_slot, neighbour_faces, remaps, borders):
    slot_count, track_extent, cross_extent, extent_z = field_now.shape
    blocks = mobility_slot.shape[0]
    minus_x = jnp.where(borders[0], field_now[:, 0], remap_face(remaps[0], neighbour_faces[0]))
    plus_x = jnp.where(borders[1], field_now[:, -1], remap_face(remaps[1], neighbour_faces[1]))
    minus_y = jnp.where(borders[2], field_now[:, :, 0], remap_face(remaps[2], neighbour_faces[2]))
    plus_y = jnp.where(borders[3], field_now[:, :, -1], remap_face(remaps[3], neighbour_faces[3]))
    laplace = jnp.concatenate([field_now[:, 1:], plus_x[:, None]], axis=1) + jnp.concatenate([minus_x[:, None], field_now[:, :-1]], axis=1)
    laplace = laplace + jnp.concatenate([field_now[:, :, 1:], plus_y[:, :, None]], axis=2) + jnp.concatenate([minus_y[:, :, None], field_now[:, :, :-1]], axis=2)
    blocked = field_now.reshape(slot_count, track_extent, cross_extent, blocks, extent_z // blocks)
    from_above = jnp.einsum("kst,txyk->sxyk", remaps[4], blocked[:, :, :, 1:, 0], precision=lax.Precision.HIGHEST)
    from_below = jnp.einsum("kts,txyk->sxyk", remaps[4], blocked[:, :, :, :-1, -1], precision=lax.Precision.HIGHEST)
    upper_rim = jnp.concatenate([from_above, blocked[:, :, :, -1:, -1]], axis=3)
    lower_rim = jnp.concatenate([blocked[:, :, :, :1, 0], from_below], axis=3)
    above = jnp.concatenate([blocked[:, :, :, :, 1:], upper_rim[..., None]], axis=4)
    below = jnp.concatenate([lower_rim[..., None], blocked[:, :, :, :, :-1]], axis=4)
    laplace = laplace + (above + below).reshape(field_now.shape) - 6.0 * field_now
    squares = jnp.sum(field_now * field_now, axis=0)
    undercool = undercool_gain * (1.0 - heat_field)
    mobility_cell = jnp.repeat(mobility_slot.T, extent_z // blocks, axis=1)[:, None, None, :]
    cubed = field_now * field_now * field_now
    change = field_now - cubed - 2.0 * mixing * field_now * (squares - field_now * field_now) + gradient_coef * laplace + undercool * field_now * (1.0 - field_now)
    return field_now + time_step * mobility_cell * change


def flatten(array):
    return array.reshape((-1,) + array.shape[2:])


def reference(order_parameter_field, reduced_warmth_ratio, entry_crystal_label, number_of_live_entries, boundary_speed_factor, heat_sheet_locator):
    piled_fragments = reduced_warmth_ratio.reshape(DEVICES, HEAT_SHEET_ROWS, SCAN_POINTS, LATERAL_POINTS)
    inverse = jnp.argsort(heat_sheet_locator).astype(jnp.int32)
    ordered = jnp.take(piled_fragments, inverse, axis=0).reshape(VERTICAL_POINTS, SCAN_POINTS, LATERAL_POINTS)
    heat_columns = ordered.reshape(VERTICAL_POINTS, XBLOCKS, BLK, YBLOCKS, BLK).transpose(1, 3, 2, 4, 0).reshape(XBLOCKS * YBLOCKS, BLK, BLK, VERTICAL_POINTS)
    mobility_slot = jnp.take(boundary_speed_factor, entry_crystal_label.astype(jnp.int32), axis=0)
    active = jnp.arange(SLOTS, dtype=jnp.int32) < number_of_live_entries[..., None]
    grain_codes = jnp.where(active, entry_crystal_label + 1, 0)
    padded = jnp.pad(grain_codes, ((1, 1), (1, 1), (0, 0), (0, 0)))
    remaps = (
        match_table(grain_codes, padded[:-2, 1:-1]),
        match_table(grain_codes, padded[2:, 1:-1]),
        match_table(grain_codes, padded[1:-1, :-2]),
        match_table(grain_codes, padded[1:-1, 2:]),
        match_table(grain_codes[:, :, :-1], grain_codes[:, :, 1:]),
    )
    flat_remaps = tuple(flatten(entry) for entry in remaps)
    flat_mobility = flatten(mobility_slot)
    live_mask = jnp.repeat(jnp.transpose(active, (0, 1, 3, 2)).astype(order_parameter_field.dtype), BLK, axis=3)
    columns = order_parameter_field.reshape(SLOTS, XBLOCKS, BLK, YBLOCKS, BLK, VERTICAL_POINTS).transpose(1, 3, 0, 2, 4, 5)
    columns = columns * live_mask[:, :, :, None, None, :]
    track_pos = jnp.broadcast_to(jnp.arange(XBLOCKS, dtype=jnp.int32)[:, None], (XBLOCKS, YBLOCKS)).reshape(-1)
    cross_pos = jnp.broadcast_to(jnp.arange(YBLOCKS, dtype=jnp.int32)[None, :], (XBLOCKS, YBLOCKS)).reshape(-1)
    borders = (track_pos == 0, track_pos == XBLOCKS - 1, cross_pos == 0, cross_pos == YBLOCKS - 1)

    def advance_one(pieces):
        return advance(pieces[0], pieces[1], pieces[2], pieces[3], pieces[4], pieces[5])

    for step_index in range(STEPS):
        empty_x = jnp.zeros_like(columns[:1, :, :, 0])
        minus_x = jnp.concatenate([empty_x, columns[:-1, :, :, -1]], axis=0)
        plus_x = jnp.concatenate([columns[1:, :, :, 0], empty_x], axis=0)
        empty_y = jnp.zeros_like(columns[:, :1, :, :, 0])
        minus_y = jnp.concatenate([empty_y, columns[:, :-1, :, :, -1]], axis=1)
        plus_y = jnp.concatenate([columns[:, 1:, :, :, 0], empty_y], axis=1)
        neighbour_faces = (flatten(minus_x), flatten(plus_x), flatten(minus_y), flatten(plus_y))
        moved = lax.map(advance_one, (flatten(columns), heat_columns, flat_mobility, neighbour_faces, flat_remaps, borders))
        columns = moved.reshape(columns.shape)
    return columns.transpose(2, 0, 3, 1, 4, 5).reshape(SLOTS, SCAN_POINTS, LATERAL_POINTS, VERTICAL_POINTS)
```

```python
import functools
import math

import jax
import jax.numpy as jnp
from jax import lax
from jax.experimental import pallas as pl
from jax.experimental.pallas import tpu as pltpu
from jax.sharding import PartitionSpec as P

MIX = 1.5
GRADIENT = 1.0
UNDERCOOL = 4.0
DT = 0.06
ROOT = math.sqrt(2.0)
MESH = pl.DeviceIdType.MESH

S = 8
B = 32
K = 4
Z = B * K
XP = B + 2
YP = B + 16
PLANE = XP * YP


def iota(dim):
    return lax.broadcasted_iota(jnp.int32, (8, Z), dim)


def kernel(
    ntx, nty,
    field_hbm, slab_hbm, label_hbm, count_hbm, speed_hbm, locator_ref,
    out_hbm,
    g0, g1, out, slab, send, recv, u_ref,
    label, count, speed,
    code, code_in, face_y, face_in,
    move, weight, q_idx, q_keep, mob, mm,
    load_sem, heat_send, heat_recv, send_sem, recv_sem, own_sem, out_sem,
):
    nd = ntx * nty
    tx, ty = lax.axis_index("track"), lax.axis_index("cross")
    me = tx * nty + ty
    lane, sub = iota(1), iota(0)

    def load(source, target, index):
        return pltpu.make_async_copy(source, target, load_sem.at[index])

    inner0 = g0.at[:, pl.ds(1, B), pl.ds(8, B), :]
    loads = (
        load(slab_hbm.at[0], slab, 0),
        load(field_hbm, inner0, 1),
        load(label_hbm, label, 2),
        load(count_hbm, count, 3),
        load(speed_hbm, speed, 4),
    )
    loads[0].start()
    barrier = pltpu.get_barrier_semaphore()

    def peers(action):
        def outer(i, carry):
            px = lax.rem(tx + i, ntx)

            def inner(j, carry):
                @pl.when(i + j > 0)
                def _():
                    action(px, lax.rem(ty + j, nty))

                return carry

            return lax.fori_loop(0, nty, inner, carry)

        lax.fori_loop(0, ntx, outer, 0)

    peers(lambda px, py: pl.semaphore_signal(barrier, inc=1, device_id=(px, py), device_id_type=MESH))
    for entry in loads[1:]:
        entry.start()

    loads[0].wait()
    group = lane // B

    def patches(px, carry):
        for half in range(nty * B // Z):
            rows = [slab[pl.ds(px * B + 8 * a, 8), pl.ds(half * Z, Z)] for a in range(4)]
            for q in range(4):
                tile = rows[q] if q == 0 else None
                parts = [rows[a] if a == q else pltpu.roll(rows[a], (B * (a - q)) % Z, axis=1) for a in range(4)]
                tile = parts[0]
                for a in range(1, 4):
                    tile = jnp.where(group == a, parts[a], tile)
                send[px * nty + half * 4 + q] = tile
        return carry

    lax.fori_loop(0, ntx, patches, 0)
    recv[me] = send[me]
    pl.semaphore_wait(barrier, nd - 1)
    peers(
        lambda px, py: pltpu.make_async_remote_copy(
            send.at[px * nty + py], recv.at[me], heat_send, heat_recv, device_id=(px, py), device_id_type=MESH
        ).start()
    )

    loads[2].wait()
    loads[3].wait()
    loads[4].wait()
    own_code = jnp.zeros((8, Z), jnp.int32)
    mobility = jnp.zeros((8, Z), jnp.float32)
    codes = []
    for k in range(K):
        row = []
        for s in range(S):
            grain = label[k * S + s]
            live = jnp.where(s < count[k], grain + 1, 0)
            row.append(live)
            here = (sub == s) & (group == k)
            own_code = jnp.where(here, live, own_code)
            mobility = jnp.where(here, speed[grain], mobility)
        codes.append(row)
    code[...] = own_code
    mob[...] = DT * mobility
    for s in range(S):
        mm[s] = jnp.broadcast_to(mob[pl.ds(s, 1), :], (8, Z))

    place = lax.rem(lane + 1, B)
    b = lax.rem(place, 2)
    slot_at = place // 2
    kk = (lane + 1) // B
    kk = jnp.where(kk == K, 0, kk)
    own_block = kk - 1 + b
    peer_block = kk - b
    have = jnp.zeros((8, Z), jnp.int32)
    for k in range(K):
        for s in range(S):
            have = jnp.where((own_block == k) & (slot_at == s), codes[k][s], have)
    index = jnp.zeros((8, Z), jnp.int32)
    keep = jnp.zeros((8, Z), jnp.float32)
    for s in range(S):
        other = jnp.zeros((8, Z), jnp.int32)
        for k in range(K):
            other = jnp.where(peer_block == k, codes[k][s], other)
        same = (other == have) & (have > 0)
        index = jnp.where(same, kk * B - b + 2 * s, index)
        keep = jnp.where(same, 1.0, keep)
    index = jnp.where(kk == 0, lane, index)
    keep = jnp.where(kk == 0, 1.0, keep)
    q_idx[...] = index
    q_keep[...] = keep

    zero = jnp.zeros((8, Z), jnp.float32)

    def clear(x, carry):
        for s in range(S):
            for g in (g0, g1):
                g[s, x, pl.ds(0, 8), :] = zero
                g[s, x, pl.ds(YP - 8, 8), :] = zero
        return carry

    lax.fori_loop(0, XP, clear, 0)
    for s in range(S):
        for g in (g0, g1):
            for x in (0, XP - 1):
                for j in range(4):
                    g[s, x, pl.ds(8 + 8 * j, 8), :] = zero
    loads[1].wait()
    scale = [
        jnp.where(jnp.broadcast_to(code[pl.ds(s, 1), :], (8, Z)) > 0, ROOT, 0.0) for s in range(S)
    ]

    def live_only(x, carry):
        for s in range(S):
            for j in range(4):
                at = (s, x, pl.ds(8 + 8 * j, 8), slice(None))
                g0[at] = g0[at] * scale[s]
        return carry

    lax.fori_loop(1, B + 1, live_only, 0)

    lower_x, upper_x = jnp.maximum(tx - 1, 0), jnp.minimum(tx + 1, ntx - 1)
    lower_y, upper_y = jnp.maximum(ty - 1, 0), jnp.minimum(ty + 1, nty - 1)
    at_end = (tx == 0, tx == ntx - 1, ty == 0, ty == nty - 1)
    target = ((lower_x, ty), (upper_x, ty), (tx, lower_y), (tx, upper_y))

    def pack_y(g, step):
        flat = g.reshape(S * PLANE, Z)

        def one(s, carry):
            for side, row in ((0, 8), (1, 8 + B - 1)):
                for x in range(0, B, 8):
                    value = flat[pl.ds(s * PLANE + (x + 1) * YP + row, 8, stride=YP), :]
                    face_y[step, side, s, pl.ds(x, 8), :] = value
            return carry

        lax.fori_loop(0, S, one, 0)

    def face(g, step, f):
        if f < 2:
            return g.at[:, (1, B)[f], pl.ds(8, B), :]
        return face_y.at[step, f - 2]

    def exchange(g, step, f):
        source, sem = face(g, step, f), step * 4 + f
        remote = pltpu.make_async_remote_copy(
            source, face_in.at[step, f ^ 1], send_sem.at[sem], recv_sem.at[sem ^ 1],
            device_id=target[f], device_id_type=MESH,
        )
        local = pltpu.make_async_copy(source, face_in.at[step, f], own_sem.at[sem])
        return remote, local

    def exchange_code(f):
        sem = 8 + f
        remote = pltpu.make_async_remote_copy(
            code, code_in.at[f ^ 1], send_sem.at[sem], recv_sem.at[sem ^ 1],
            device_id=target[f], device_id_type=MESH,
        )
        local = pltpu.make_async_copy(code, code_in.at[f], own_sem.at[sem])
        return remote, local

    def begin(pair, f):
        @pl.when(jnp.logical_not(at_end[f]))
        def _():
            pair[0].start()

        @pl.when(at_end[f])
        def _():
            pair[1].start()

    def finish(pair_sent, pair_got, f):
        @pl.when(jnp.logical_not(at_end[f]))
        def _():
            pair_sent[0].wait_send()
            pair_got[0].wait_recv()

        @pl.when(at_end[f])
        def _():
            pair_sent[1].wait()

    pack_y(g0, 0)
    for f in range(4):
        begin(exchange_code(f), f)
        begin(exchange(g0, 0, f), f)

    rim_low = lax.rem(lane, B) == 0
    rim_high = lax.rem(lane, B) == B - 1
    in_pack = [slot_at == s for s in range(S)]

    def neighbours(g, x, j):
        row = 8 + 8 * j
        own = [g[s, x, pl.ds(row, 8), :] for s in range(S)]
        squares = own[0] * own[0]
        packed = own[0]
        for s in range(1, S):
            squares = squares + own[s] * own[s]
            packed = jnp.where(in_pack[s], pltpu.roll(own[s], 2 * s, axis=1), packed)
        rim = jnp.take_along_axis(packed, q_idx[...], axis=1) * q_keep[...]
        sums = []
        for s in range(S):
            back = rim if s == 0 else pltpu.roll(rim, Z - 2 * s, axis=1)
            below = jnp.where(rim_low, back, pltpu.roll(own[s], 1, axis=1))
            above = jnp.where(rim_high, back, pltpu.roll(own[s], Z - 1, axis=1))
            total = g[s, x - 1, pl.ds(row, 8), :] + g[s, x + 1, pl.ds(row, 8), :]
            total = total + (g[s, x, pl.ds(row - 1, 8), :] + g[s, x, pl.ds(row + 1, 8), :])
            sums.append(total + (below + above))
        return own, squares, sums

    def first_sweep(x, carry):
        for j in range(4):
            own, squares, sums = neighbours(g0, x, j)
            level = (1.0 - 6.0 * GRADIENT) - MIX * squares
            for s in range(S):
                change = own[s] * (level + own[s] * own[s]) + sums[s]
                g1[s, x, pl.ds(8 + 8 * j, 8), :] = own[s] + mm[s] * change
        return carry

    lax.fori_loop(1, B + 1, first_sweep, 0)

    for f in range(4):
        finish(exchange_code(f), exchange_code(f ^ 1), f)
        index = jnp.zeros((8, Z), jnp.int32)
        value = jnp.zeros((8, Z), jnp.float32)
        own_now = code[...]
        for s in range(S):
            other = jnp.broadcast_to(code_in[f, pl.ds(s, 1), :], (8, Z))
            same = (other == own_now) & (own_now > 0)
            index = jnp.where(same, s, index)
            value = jnp.where(same, mob[...], value)
        move[f] = index
        weight[f] = value

    def add_faces(g, base, stride_s, stride_x, first_x, first_y, step, factor, f):
        finish(exchange(g, step, f), exchange(g, step, f ^ 1), f)
        flat = base.reshape(S * stride_s, Z)
        source = face_in.at[step, f].reshape(S * B, Z)
        turn, gain = move[f], weight[f] * factor

        def one(i, carry):
            got = jnp.take_along_axis(source[pl.ds(i, 8, stride=B), :], turn, axis=0)
            if f < 2:
                row = (first_x + (0, B - 1)[f]) * stride_x + first_y + i
            else:
                row = (first_x + i) * stride_x + first_y + (0, B - 1)[f - 2]
            at = (pl.ds(row, 8, stride=stride_s), slice(None))
            flat[at] = flat[at] + gain * got
            return carry

        lax.fori_loop(0, B, one, 0, unroll=4)

    for f in range(4):
        add_faces(g0, g1, PLANE, YP, 1, 8, 0, 1.0, f)

    everyone = pltpu.make_async_remote_copy(
        send.at[pl.ds(0, nd - 1)], recv.at[pl.ds(0, nd - 1)], heat_send, heat_recv,
        device_id=(tx, ty), device_id_type=MESH,
    )
    everyone.wait_send()
    everyone.wait_recv()
    locator = jnp.broadcast_to(locator_ref[...], (Z, Z))
    order = jnp.where(locator == lax.broadcasted_iota(jnp.int32, (Z, Z), 0), 1.0, 0.0).astype(jnp.bfloat16)
    flat_recv = recv.reshape(nd * 8, Z)
    for s in range(8):
        value = (UNDERCOOL / ROOT) * (1.0 - flat_recv[pl.ds(s, nd, stride=8), :])
        value = jnp.transpose(value)
        high = value.astype(jnp.bfloat16)
        low = (value - high.astype(jnp.float32)).astype(jnp.bfloat16)
        dims = (((1,), (1,)), ((), ()))
        placed = lax.dot_general(high, order, dims, preferred_element_type=jnp.float32)
        placed = placed + lax.dot_general(low, order, dims, preferred_element_type=jnp.float32)
        for a in range(4):
            u_ref[pl.ds((8 * a + s) * B, B), :] = placed[a * B : (a + 1) * B]

    def heat_term(x, tiles):
        for j in tiles:
            u = u_ref[pl.ds((x - 1) * B + 8 * j, 8), :]
            for s in range(S):
                at = (s, x, pl.ds(8 + 8 * j, 8), slice(None))
                own = g0[at]
                g1[at] = g1[at] + (mm[s] * u) * (own * (ROOT - own))

    def heat_loop(tiles):
        def body(x, carry):
            heat_term(x, tiles)
            return carry

        lax.fori_loop(2, B, body, 0)

    heat_term(1, range(4))
    heat_term(B, range(4))
    for f in (0, 1):
        begin(exchange(g1, 1, f), f)
    heat_loop((0, 3))
    pack_y(g1, 1)
    for f in (2, 3):
        begin(exchange(g1, 1, f), f)
    heat_loop((1, 2))

    def second_sweep(x, carry):
        for j in range(4):
            own, squares, sums = neighbours(g1, x, j)
            u = u_ref[pl.ds((x - 1) * B + 8 * j, 8), :]
            level = (1.0 - 6.0 * GRADIENT) + ROOT * u - MIX * squares
            for s in range(S):
                change = own[s] * (level + own[s] * (own[s] - u)) + sums[s]
                out[s, x - 1, pl.ds(8 * j, 8), :] = (1.0 / ROOT) * (own[s] + mm[s] * change)
        return carry

    lax.fori_loop(1, B + 1, second_sweep, 0)
    for f in range(4):
        add_faces(g1, out, B * B, B, 0, 0, 1, 1.0 / ROOT, f)
    store = pltpu.make_async_copy(out, out_hbm, out_sem)
    store.start()
    store.wait()


def on_device(ntx, nty, field, heat, label, count, speed, locator):
    nd = ntx * nty
    any_space = pl.BlockSpec(memory_space=pl.ANY)
    return pl.pallas_call(
        functools.partial(kernel, ntx, nty),
        out_shape=jax.ShapeDtypeStruct(field.shape, jnp.float32),
        in_specs=[any_space] * 5 + [pl.BlockSpec(memory_space=pltpu.VMEM)],
        out_specs=any_space,
        scratch_shapes=[
            pltpu.VMEM((S, XP, YP, Z), jnp.float32),
            pltpu.VMEM((S, XP, YP, Z), jnp.float32),
            pltpu.VMEM((S, B, B, Z), jnp.float32),
            pltpu.VMEM(heat.shape[1:], jnp.float32),
            pltpu.VMEM((nd, 8, Z), jnp.float32),
            pltpu.VMEM((nd, 8, Z), jnp.float32),
            pltpu.VMEM((B * B, Z), jnp.float32),
            pltpu.SMEM((K * S,), jnp.int32),
            pltpu.SMEM((K,), jnp.int32),
            pltpu.SMEM(speed.shape, jnp.float32),
            pltpu.VMEM((8, Z), jnp.int32),
            pltpu.VMEM((4, 8, Z), jnp.int32),
            pltpu.VMEM((2, 2, S, B, Z), jnp.float32),
            pltpu.VMEM((2, 4, S, B, Z), jnp.float32),
            pltpu.VMEM((4, 8, Z), jnp.int32),
            pltpu.VMEM((4, 8, Z), jnp.float32),
            pltpu.VMEM((8, Z), jnp.int32),
            pltpu.VMEM((8, Z), jnp.float32),
            pltpu.VMEM((8, Z), jnp.float32),
            pltpu.VMEM((S, 8, Z), jnp.float32),
            pltpu.SemaphoreType.DMA((5,)),
            pltpu.SemaphoreType.DMA,
            pltpu.SemaphoreType.DMA,
            pltpu.SemaphoreType.DMA((12,)),
            pltpu.SemaphoreType.DMA((12,)),
            pltpu.SemaphoreType.DMA((12,)),
            pltpu.SemaphoreType.DMA,
        ],
        compiler_params=pltpu.CompilerParams(
            collective_id=0, has_side_effects=True, vmem_limit_bytes=60 * 2**20
        ),
        name="grains",
    )(
        field,
        heat,
        label.reshape(K * S),
        count.reshape(K),
        speed,
        locator.reshape(1, Z),
    )


def solution(mesh):
    ntx, nty = mesh.shape["track"], mesh.shape["cross"]
    return jax.shard_map(
        functools.partial(on_device, ntx, nty),
        mesh=mesh,
        in_specs=(
            P(None, "track", "cross", None),
            P(("track", "cross"), None, None),
            P("track", "cross", None, None),
            P("track", "cross", None),
            P(),
            P(),
        ),
        out_specs=P(None, "track", "cross", None),
        check_vma=False,
    )
```

```python
import functools
import math

import jax
import jax.numpy as jnp
from jax import lax
from jax.experimental import pallas as pl
from jax.experimental.pallas import tpu as pltpu
from jax.sharding import PartitionSpec as P

MIX = 1.5
GRADIENT = 1.0
UNDERCOOL = 4.0
DT = 0.06
ROOT = math.sqrt(2.0)
MESH = pl.DeviceIdType.MESH

S = 8
B = 32
K = 4
Z = B * K
XP = B + 2
YP = B + 16
PLANE = XP * YP
PIECE = 2
CHUNK = 8


def iota(dim):
    return lax.broadcasted_iota(jnp.int32, (8, Z), dim)


def kernel(
    ntx, nty,
    field_hbm, slab_hbm, label_hbm, count_hbm, speed_hbm, locator_hbm,
    out, order_out,
    raw, g0, g1, slab, send, recv, u_ref, split, couple,
    label, count, speed, locator_ref,
    code, code_in, face_y, face_in,
    move, weight, mob, mm,
    load_sem, heat_send, heat_recv, send_sem, recv_sem, own_sem,
):
    nd = ntx * nty
    tx, ty = lax.axis_index("track"), lax.axis_index("cross")
    me = tx * nty + ty
    lane, sub = iota(1), iota(0)

    def load(source, target, index):
        return pltpu.make_async_copy(source, target, load_sem.at[index])

    loads = (
        load(slab_hbm.at[0], slab, 0),
        load(field_hbm, raw, 1),
        load(label_hbm, label, 2),
        load(count_hbm, count, 3),
        load(speed_hbm, speed, 4),
        load(locator_hbm, locator_ref, 5),
    )
    loads[0].start()
    barrier = pltpu.get_barrier_semaphore()

    def peers(action):
        def outer(i, carry):
            px = lax.rem(tx + i, ntx)

            def inner(j, carry):
                @pl.when(i + j > 0)
                def _():
                    action(px, lax.rem(ty + j, nty))

                return carry

            return lax.fori_loop(0, nty, inner, carry)

        lax.fori_loop(0, ntx, outer, 0)

    peers(lambda px, py: pl.semaphore_signal(barrier, inc=1, device_id=(px, py), device_id_type=MESH))
    for entry in loads[1:]:
        entry.start()

    loads[0].wait()
    group = lane // B

    def patches(px, carry):
        for half in range(nty * B // Z):
            rows = [slab[pl.ds(px * B + 8 * a, 8), pl.ds(half * Z, Z)] for a in range(4)]
            for q in range(4):
                tile = rows[q] if q == 0 else None
                parts = [rows[a] if a == q else pltpu.roll(rows[a], (B * (a - q)) % Z, axis=1) for a in range(4)]
                tile = parts[0]
                for a in range(1, 4):
                    tile = jnp.where(group == a, parts[a], tile)
                send[px * nty + half * 4 + q] = tile
        return carry

    lax.fori_loop(0, ntx, patches, 0)
    recv[me] = send[me]
    pl.semaphore_wait(barrier, nd - 1)
    peers(
        lambda px, py: pltpu.make_async_remote_copy(
            send.at[px * nty + py], recv.at[me], heat_send, heat_recv, device_id=(px, py), device_id_type=MESH
        ).start()
    )

    loads[2].wait()
    loads[3].wait()
    loads[4].wait()
    loads[5].wait()
    codes, orders, matches = [], [], []
    for k in range(K):
        live = [jnp.where(s < count[0, 0, k], label[0, 0, k, s] + 1, 0) for s in range(S)]
        if k == 0:
            order, code_at, matched = [jnp.int32(s) for s in range(S)], live, None
        else:
            bits = []
            for j in range(S):
                bit = jnp.int32(0)
                for p in range(S):
                    bit = jnp.where((live[j] == codes[k - 1][p]) & (live[j] > 0), 1 << p, bit)
                bits.append(bit)
            matched = functools.reduce(jnp.bitwise_or, bits)
            free = matched ^ (2**S - 1)
            for j in range(S):
                low = free & -free
                free = jnp.where(bits[j] == 0, free ^ low, free)
                bits[j] = jnp.where(bits[j] == 0, low, bits[j])
            order, code_at = [], []
            for p in range(S):
                slot, here = jnp.int32(0), live[0]
                for j in range(1, S):
                    slot = jnp.where(bits[j] == 1 << p, j, slot)
                    here = jnp.where(bits[j] == 1 << p, live[j], here)
                order.append(slot)
                code_at.append(here)
            for j in range(S):
                place = jnp.int32(0)
                for p in range(1, S):
                    place = jnp.where(bits[j] == 1 << p, p, place)
                order_out[k, j] = place
        if k == 0:
            for j in range(S):
                order_out[k, j] = j
        codes.append(code_at)
        orders.append(order)
        matches.append(matched)
    own_code = jnp.zeros((8, Z), jnp.int32)
    mobility = jnp.zeros((8, Z), jnp.float32)
    for k in range(K):
        for s in range(S):
            here = (sub == s) & (group == k)
            own_code = jnp.where(here, codes[k][s], own_code)
            mobility = jnp.where(here, speed[label[0, 0, k, orders[k][s]]], mobility)
    code[...] = own_code
    mob[...] = DT * mobility
    for s in range(S):
        mm[s] = jnp.broadcast_to(mob[pl.ds(s, 1), :], (8, Z))

    wide = lax.broadcasted_iota(jnp.int32, (Z, Z), 1)
    deep = lax.broadcasted_iota(jnp.int32, (Z, Z), 0)
    beside = (deep == wide - 1) | (deep == wide + 1) | ((deep == wide) & ((wide == 0) | (wide == Z - 1)))
    edge = jnp.maximum(deep, wide)
    crossing = (deep != wide) & (lax.rem(edge, B) == 0)
    base_matrix = jnp.where(beside & jnp.logical_not(crossing), 1.0, 0.0)
    crossings = [jnp.where(beside & crossing & (edge == k * B), 1.0, 0.0) for k in range(1, K)]
    for s in range(S):
        matrix = base_matrix
        for k in range(1, K):
            matrix = matrix + jnp.where((matches[k] & (1 << s)) > 0, crossings[k - 1], 0.0)
        matrix = matrix.astype(jnp.bfloat16)
        couple[s, pl.ds(0, Z), :] = matrix
        couple[s, pl.ds(Z, Z), :] = matrix

    zero = jnp.zeros((8, Z), jnp.float32)

    def clear(x, carry):
        for s in range(S):
            for g in (g0, g1):
                g[s, x, pl.ds(0, 8), :] = zero
                g[s, x, pl.ds(YP - 8, 8), :] = zero
        return carry

    lax.fori_loop(0, XP, clear, 0)
    for s in range(S):
        for g in (g0, g1):
            for x in (0, XP - 1):
                for j in range(4):
                    g[s, x, pl.ds(8 + 8 * j, 8), :] = zero
    loads[1].wait()
    wide_group = lax.broadcasted_iota(jnp.int32, (16, Z), 1) // B
    scale = [
        jnp.where(jnp.broadcast_to(code[pl.ds(s, 1), :], (16, Z)) > 0, ROOT, 0.0) for s in range(S)
    ]

    def keep_split(s, row, value):
        high = value.astype(jnp.bfloat16)
        split[s, pl.ds(row, 16), pl.ds(0, Z)] = high
        split[s, pl.ds(row, 16), pl.ds(Z, Z)] = (value - high.astype(jnp.float32)).astype(jnp.bfloat16)

    def place_field(x, carry):
        for s in range(S):
            for j in range(0, 4, 2):
                rows = pl.ds(8 * j, 16)
                value = raw[s, x, rows, :]
                for k in range(1, K):
                    value = jnp.where(wide_group == k, raw[orders[k][s], x, rows, :], value)
                value = value * scale[s]
                g0[s, x + 1, pl.ds(8 + 8 * j, 16), :] = value
                keep_split(s, pl.multiple_of(x * B, B) + 8 * j, value)
        return carry

    lax.fori_loop(0, B, place_field, 0)

    lower_x, upper_x = jnp.maximum(tx - 1, 0), jnp.minimum(tx + 1, ntx - 1)
    lower_y, upper_y = jnp.maximum(ty - 1, 0), jnp.minimum(ty + 1, nty - 1)
    at_end = (tx == 0, tx == ntx - 1, ty == 0, ty == nty - 1)
    target = ((lower_x, ty), (upper_x, ty), (tx, lower_y), (tx, upper_y))

    def pack_y(g, step):
        flat = g.reshape(S * PLANE, Z)

        def one(s, carry):
            for side, row in ((0, 8), (1, 8 + B - 1)):
                for x in range(0, B, 8):
                    value = flat[pl.ds(s * PLANE + (x + 1) * YP + row, 8, stride=YP), :]
                    face_y[step, side, s, pl.ds(x, 8), :] = value
            return carry

        lax.fori_loop(0, S, one, 0)

    def face(g, step, f):
        if f < 2:
            return g.at[:, (1, B)[f], pl.ds(8, B), :]
        return face_y.at[step, f - 2]

    def exchange(g, step, f):
        source, sem = face(g, step, f), step * 4 + f
        remote = pltpu.make_async_remote_copy(
            source, face_in.at[step, f ^ 1], send_sem.at[sem], recv_sem.at[sem ^ 1],
            device_id=target[f], device_id_type=MESH,
        )
        local = pltpu.make_async_copy(source, face_in.at[step, f], own_sem.at[sem])
        return remote, local

    def exchange_code(f):
        sem = 8 + f
        remote = pltpu.make_async_remote_copy(
            code, code_in.at[f ^ 1], send_sem.at[sem], recv_sem.at[sem ^ 1],
            device_id=target[f], device_id_type=MESH,
        )
        local = pltpu.make_async_copy(code, code_in.at[f], own_sem.at[sem])
        return remote, local

    def begin(pair, f):
        @pl.when(jnp.logical_not(at_end[f]))
        def _():
            pair[0].start()

        @pl.when(at_end[f])
        def _():
            pair[1].start()

    def finish(pair_sent, pair_got, f):
        @pl.when(jnp.logical_not(at_end[f]))
        def _():
            pair_sent[0].wait_send()
            pair_got[0].wait_recv()

        @pl.when(at_end[f])
        def _():
            pair_sent[1].wait()

    pack_y(g0, 0)
    for f in range(4):
        begin(exchange_code(f), f)
        begin(exchange(g0, 0, f), f)

    def sweep(g, i, use):
        rows = pl.ds(pl.multiple_of(i * CHUNK * B, CHUNK * B), CHUNK * B)
        depth = [
            lax.dot_general(
                split[s, rows, :], couple[s], (((1,), (0,)), ((), ())), preferred_element_type=jnp.float32
            )
            for s in range(S)
        ]
        for part in range(CHUNK):
            x = i * CHUNK + part + 1
            for j in range(4):
                row = 8 + 8 * j
                own = [g[s, x, pl.ds(row, 8), :] for s in range(S)]
                squares = own[0] * own[0]
                for s in range(1, S):
                    squares = squares + own[s] * own[s]
                sums = []
                for s in range(S):
                    total = g[s, x - 1, pl.ds(row, 8), :] + g[s, x + 1, pl.ds(row, 8), :]
                    total = total + (g[s, x, pl.ds(row - 1, 8), :] + g[s, x, pl.ds(row + 1, 8), :])
                    sums.append(total + depth[s][part * B + 8 * j : part * B + 8 * j + 8])
                use(x, j, own, squares, sums)

    def first(x, j, own, squares, sums):
        level = (1.0 - 6.0 * GRADIENT) - MIX * squares
        for s in range(S):
            change = own[s] * (level + own[s] * own[s]) + sums[s]
            g1[s, x, pl.ds(8 + 8 * j, 8), :] = own[s] + mm[s] * change

    def first_sweep(i, carry):
        sweep(g0, i, first)
        return carry

    lax.fori_loop(0, B // CHUNK, first_sweep, 0)

    for f in range(4):
        finish(exchange_code(f), exchange_code(f ^ 1), f)
        index = jnp.zeros((8, Z), jnp.int32)
        value = jnp.zeros((8, Z), jnp.float32)
        own_now = code[...]
        for s in range(S):
            other = jnp.broadcast_to(code_in[f, pl.ds(s, 1), :], (8, Z))
            same = (other == own_now) & (own_now > 0)
            index = jnp.where(same, s, index)
            value = jnp.where(same, mob[...], value)
        move[f] = index
        weight[f] = value

    def add_faces(g, base, stride_s, stride_x, first_x, first_y, step, factor, f):
        finish(exchange(g, step, f), exchange(g, step, f ^ 1), f)
        flat = base.reshape(S * stride_s, Z)
        source = face_in.at[step, f].reshape(S * B, Z)
        turn, gain = move[f], weight[f] * factor

        def one(i, carry):
            got = jnp.take_along_axis(source[pl.ds(i, 8, stride=B), :], turn, axis=0)
            if f < 2:
                row = (first_x + (0, B - 1)[f]) * stride_x + first_y + i
            else:
                row = (first_x + i) * stride_x + first_y + (0, B - 1)[f - 2]
            at = (pl.ds(row, 8, stride=stride_s), slice(None))
            flat[at] = flat[at] + gain * got
            return carry

        lax.fori_loop(0, B, one, 0, unroll=4)

    for f in range(4):
        add_faces(g0, g1, PLANE, YP, 1, 8, 0, 1.0, f)

    everyone = pltpu.make_async_remote_copy(
        send.at[pl.ds(0, nd - 1)], recv.at[pl.ds(0, nd - 1)], heat_send, heat_recv,
        device_id=(tx, ty), device_id_type=MESH,
    )
    everyone.wait_send()
    everyone.wait_recv()
    locator = jnp.broadcast_to(locator_ref[...], (Z, Z))
    order = jnp.where(locator == lax.broadcasted_iota(jnp.int32, (Z, Z), 0), 1.0, 0.0).astype(jnp.bfloat16)
    flat_recv = recv.reshape(nd * 8, Z)
    for s in range(8):
        value = (UNDERCOOL / ROOT) * (1.0 - flat_recv[pl.ds(s, nd, stride=8), :])
        value = jnp.transpose(value)
        high = value.astype(jnp.bfloat16)
        low = (value - high.astype(jnp.float32)).astype(jnp.bfloat16)
        dims = (((1,), (1,)), ((), ()))
        placed = lax.dot_general(high, order, dims, preferred_element_type=jnp.float32)
        placed = placed + lax.dot_general(low, order, dims, preferred_element_type=jnp.float32)
        for a in range(4):
            u_ref[pl.ds((8 * a + s) * B, B), :] = placed[a * B : (a + 1) * B]

    def heat_term(x, pairs):
        for j in pairs:
            u = u_ref[pl.ds((x - 1) * B + 8 * j, 16), :]
            for s in range(S):
                at = (s, x, pl.ds(8 + 8 * j, 16), slice(None))
                own = g0[at]
                gain = jnp.concatenate([mm[s], mm[s]], axis=0)
                value = g1[at] + (gain * u) * (own * (ROOT - own))
                g1[at] = value
                keep_split(s, pl.multiple_of((x - 1) * B, B) + 8 * j, value)

    heat_term(1, (0, 2))
    heat_term(B, (0, 2))
    for f in (0, 1):
        begin(exchange(g1, 1, f), f)

    def heat_rest(x, carry):
        heat_term(x, (0, 2))
        return carry

    lax.fori_loop(2, B, heat_rest, 0)
    pack_y(g1, 1)
    for f in (2, 3):
        begin(exchange(g1, 1, f), f)

    def second(x, j, own, squares, sums):
        u = u_ref[pl.ds((x - 1) * B + 8 * j, 8), :]
        level = (1.0 - 6.0 * GRADIENT) + ROOT * u - MIX * squares
        for s in range(S):
            change = own[s] * (level + own[s] * (own[s] - u)) + sums[s]
            out[s, x - 1, pl.ds(8 * j, 8), :] = own[s] + mm[s] * change

    def second_sweep(i, carry):
        sweep(g1, i, second)
        return carry

    lax.fori_loop(0, B // CHUNK, second_sweep, 0)
    for f in range(4):
        add_faces(g1, out, B * B, B, 0, 0, 1, 1.0, f)


def restore(order, moved, result_hbm, result, out_sem):
    group = lax.broadcasted_iota(jnp.int32, (8, Z), 1) // B
    places = [[order[k, s] for s in range(S)] for k in range(K)]

    def piece(i):
        planes = pl.ds(i * PIECE, PIECE)
        return pltpu.make_async_copy(result.at[:, planes], result_hbm.at[:, planes], out_sem)

    def plane(x):
        values = []
        for s in range(S):
            for j in range(4):
                rows = pl.ds(8 * j, 8)
                value = moved[s, x, rows, :]
                for k in range(1, K):
                    value = jnp.where(group == k, moved[places[k][s], x, rows, :], value)
                values.append(value * (1.0 / ROOT))
        for s in range(S):
            for j in range(4):
                result[s, x, pl.ds(8 * j, 8), :] = values[4 * s + j]

    def one(i, carry):
        for x in range(PIECE):
            plane(i * PIECE + x)
        piece(i).start()
        return carry

    lax.fori_loop(0, B // PIECE, one, 0)
    pltpu.make_async_copy(result, result_hbm, out_sem).wait()


def on_device(ntx, nty, field, heat, label, count, speed, locator):
    nd = ntx * nty
    in_hbm = pl.BlockSpec(memory_space=pltpu.HBM)
    f32, i32 = jnp.float32, jnp.int32
    moved, order = pl.pallas_call(
        functools.partial(kernel, ntx, nty),
        out_shape=(pltpu.VMEM(field.shape, f32), pltpu.SMEM((K, S), i32)),
        in_specs=[in_hbm] * 6,
        out_specs=(pl.BlockSpec(memory_space=pltpu.VMEM), pl.BlockSpec(memory_space=pltpu.SMEM)),
        scratch_shapes=[
            pltpu.VMEM((S, B, B, Z), f32),
            pltpu.VMEM((S, XP, YP, Z), f32),
            pltpu.VMEM((S, XP, YP, Z), f32),
            pltpu.VMEM(heat.shape[1:], f32),
            pltpu.VMEM((nd, 8, Z), f32),
            pltpu.VMEM((nd, 8, Z), f32),
            pltpu.VMEM((B * B, Z), f32),
            pltpu.VMEM((S, B * B, 2 * Z), jnp.bfloat16),
            pltpu.VMEM((S, 2 * Z, Z), jnp.bfloat16),
            pltpu.SMEM(label.shape, i32),
            pltpu.SMEM(count.shape, i32),
            pltpu.SMEM(speed.shape, f32),
            pltpu.VMEM((1, Z), i32),
            pltpu.VMEM((8, Z), i32),
            pltpu.VMEM((4, 8, Z), i32),
            pltpu.VMEM((2, 2, S, B, Z), f32),
            pltpu.VMEM((2, 4, S, B, Z), f32),
            pltpu.VMEM((4, 8, Z), i32),
            pltpu.VMEM((4, 8, Z), f32),
            pltpu.VMEM((8, Z), f32),
            pltpu.VMEM((S, 8, Z), f32),
            pltpu.SemaphoreType.DMA((6,)),
            pltpu.SemaphoreType.DMA,
            pltpu.SemaphoreType.DMA,
            pltpu.SemaphoreType.DMA((12,)),
            pltpu.SemaphoreType.DMA((12,)),
            pltpu.SemaphoreType.DMA((12,)),
        ],
        compiler_params=pltpu.CompilerParams(
            collective_id=0, has_side_effects=True, vmem_limit_bytes=59 * 2**20
        ),
        name="grains",
    )(field, heat, label, count, speed, locator.reshape(1, Z))
    return pl.pallas_call(
        restore,
        out_shape=jax.ShapeDtypeStruct(field.shape, f32),
        in_specs=[pl.BlockSpec(memory_space=pltpu.SMEM), pl.BlockSpec(memory_space=pltpu.VMEM)],
        out_specs=in_hbm,
        scratch_shapes=[
            pltpu.VMEM(field.shape, f32),
            pltpu.SemaphoreType.DMA,
        ],
        compiler_params=pltpu.CompilerParams(vmem_limit_bytes=32 * 2**20),
        name="restore",
    )(order, moved)


def solution(mesh):
    ntx, nty = mesh.shape["track"], mesh.shape["cross"]
    return jax.shard_map(
        functools.partial(on_device, ntx, nty),
        mesh=mesh,
        in_specs=(
            P(None, "track", "cross", None),
            P(("track", "cross"), None, None),
            P("track", "cross", None, None),
            P("track", "cross", None),
            P(),
            P(),
        ),
        out_specs=P(None, "track", "cross", None),
        check_vma=False,
    )
```

```python
import functools
import math

import jax
import jax.numpy as jnp
from jax import lax
from jax.experimental import pallas as pl
from jax.experimental.pallas import tpu as pltpu
from jax.sharding import PartitionSpec as P

MIX = 1.5
GRADIENT = 1.0
UNDERCOOL = 4.0
DT = 0.06
ROOT = math.sqrt(2.0)
MESH = pl.DeviceIdType.MESH

S = 8
B = 32
K = 4
Z = B * K
XP = B + 2
YP = B + 16
PLANE = XP * YP
PIECE = 2
CHUNK = 8


def iota(dim):
    return lax.broadcasted_iota(jnp.int32, (8, Z), dim)


def kernel(
    ntx, nty,
    field_hbm, slab_hbm, label_hbm, count_hbm, speed_hbm, locator_hbm,
    out, order_out,
    raw, g0, g1, slab, send, recv, u_ref, split, couple,
    label, count, speed, locator_ref,
    code, code_in, face_y, face_in,
    move, weight, mob, mm,
    load_sem, heat_send, heat_recv, send_sem, recv_sem, own_sem,
):
    nd = ntx * nty
    tx, ty = lax.axis_index("track"), lax.axis_index("cross")
    me = tx * nty + ty
    lane, sub = iota(1), iota(0)

    def load(source, target, index):
        return pltpu.make_async_copy(source, target, load_sem.at[index])

    loads = (
        load(slab_hbm.at[0], slab, 0),
        load(field_hbm, raw, 1),
        load(label_hbm, label, 2),
        load(count_hbm, count, 3),
        load(speed_hbm, speed, 4),
        load(locator_hbm, locator_ref, 5),
    )
    loads[0].start()
    barrier = pltpu.get_barrier_semaphore()

    def peers(action):
        def outer(i, carry):
            px = lax.rem(tx + i, ntx)

            def inner(j, carry):
                @pl.when(i + j > 0)
                def _():
                    action(px, lax.rem(ty + j, nty))

                return carry

            return lax.fori_loop(0, nty, inner, carry)

        lax.fori_loop(0, ntx, outer, 0)

    peers(lambda px, py: pl.semaphore_signal(barrier, inc=1, device_id=(px, py), device_id_type=MESH))
    for entry in loads[1:]:
        entry.start()

    loads[0].wait()
    group = lane // B

    def patches(px, carry):
        for half in range(nty * B // Z):
            rows = [slab[pl.ds(px * B + 8 * a, 8), pl.ds(half * Z, Z)] for a in range(4)]
            for q in range(4):
                tile = rows[q] if q == 0 else None
                parts = [rows[a] if a == q else pltpu.roll(rows[a], (B * (a - q)) % Z, axis=1) for a in range(4)]
                tile = parts[0]
                for a in range(1, 4):
                    tile = jnp.where(group == a, parts[a], tile)
                send[px * nty + half * 4 + q] = tile
        return carry

    lax.fori_loop(0, ntx, patches, 0)
    recv[me] = send[me]

    lower_x, upper_x = jnp.maximum(tx - 1, 0), jnp.minimum(tx + 1, ntx - 1)
    lower_y, upper_y = jnp.maximum(ty - 1, 0), jnp.minimum(ty + 1, nty - 1)
    at_end = (tx == 0, tx == ntx - 1, ty == 0, ty == nty - 1)
    target = ((lower_x, ty), (upper_x, ty), (tx, lower_y), (tx, upper_y))

    def face(step, f):
        if f >= 2:
            return face_y.at[step, f - 2]
        if step == 0:
            return field_hbm.at[:, (0, B - 1)[f]]
        return g1.at[:, (1, B)[f], pl.ds(8, B), :]

    def to_peer(step, f):
        if step == 2:
            source, here, there = code, code_in.at[f], code_in.at[f ^ 1]
        else:
            source, here, there = face(step, f), face_in.at[step, f], face_in.at[step, f ^ 1]
        sem = step * 4 + f
        remote = functools.partial(
            pltpu.make_async_remote_copy,
            source, there, send_sem.at[sem], recv_sem.at[sem ^ 1], device_id=target[f], device_id_type=MESH,
        )
        local = functools.partial(pltpu.make_async_copy, source, here, own_sem.at[sem])
        return remote, local

    def begin(step, f):
        remote, local = to_peer(step, f)

        @pl.when(jnp.logical_not(at_end[f]))
        def _():
            remote().start()

        @pl.when(at_end[f])
        def _():
            local().start()

    def finish(step, f):
        remote, local = to_peer(step, f)
        back, _ = to_peer(step, f ^ 1)

        @pl.when(jnp.logical_not(at_end[f]))
        def _():
            remote().wait_send()
            back().wait_recv()

        @pl.when(at_end[f])
        def _():
            local().wait()

    loads[1].wait()
    flat_raw = raw.reshape(S * B * B, Z)

    def pack_raw(s, carry):
        for side, row in ((0, 0), (1, B - 1)):
            values = [flat_raw[pl.ds((s * B + x) * B + row, 8, stride=B), :] for x in range(0, B, 8)]
            for x in range(0, B, 8):
                face_y[0, side, s, pl.ds(x, 8), :] = values[x // 8]
        return carry

    lax.fori_loop(0, S, pack_raw, 0)
    pl.semaphore_wait(barrier, nd - 1)
    peers(
        lambda px, py: pltpu.make_async_remote_copy(
            send.at[px * nty + py], recv.at[me], heat_send, heat_recv, device_id=(px, py), device_id_type=MESH
        ).start()
    )
    begin(0, 2)
    begin(0, 3)
    begin(0, 0)
    begin(0, 1)

    loads[2].wait()
    loads[3].wait()
    loads[4].wait()
    loads[5].wait()
    lives, codes, orders, matches = [], [], [], []
    for k in range(K):
        live = [jnp.where(s < count[0, 0, k], label[0, 0, k, s] + 1, 0) for s in range(S)]
        if k == 0:
            order, code_at, matched = [jnp.int32(s) for s in range(S)], live, None
        else:
            bits = []
            for j in range(S):
                bit = jnp.int32(0)
                for p in range(S):
                    bit = jnp.where((live[j] == codes[k - 1][p]) & (live[j] > 0), 1 << p, bit)
                bits.append(bit)
            matched = functools.reduce(jnp.bitwise_or, bits)
            free = matched ^ (2**S - 1)
            for j in range(S):
                low = free & -free
                free = jnp.where(bits[j] == 0, free ^ low, free)
                bits[j] = jnp.where(bits[j] == 0, low, bits[j])
            order, code_at = [], []
            for p in range(S):
                slot, here = jnp.int32(0), live[0]
                for j in range(1, S):
                    slot = jnp.where(bits[j] == 1 << p, j, slot)
                    here = jnp.where(bits[j] == 1 << p, live[j], here)
                order.append(slot)
                code_at.append(here)
            for j in range(S):
                place = jnp.int32(0)
                for p in range(1, S):
                    place = jnp.where(bits[j] == 1 << p, p, place)
                order_out[k, j] = place
        if k == 0:
            for j in range(S):
                order_out[k, j] = j
        lives.append(live)
        codes.append(code_at)
        orders.append(order)
        matches.append(matched)
    own_code = jnp.zeros((8, Z), jnp.int32)
    listed = jnp.zeros((8, Z), jnp.int32)
    mobility = jnp.zeros((8, Z), jnp.float32)
    for k in range(K):
        for s in range(S):
            here = (sub == s) & (group == k)
            own_code = jnp.where(here, codes[k][s], own_code)
            listed = jnp.where(here, lives[k][s], listed)
            mobility = jnp.where(here, speed[label[0, 0, k, orders[k][s]]], mobility)
    code[0] = listed
    code[1] = own_code
    for f in range(4):
        begin(2, f)
    mob[...] = DT * mobility
    for s in range(S):
        mm[s] = jnp.broadcast_to(mob[pl.ds(s, 1), :], (8, Z))

    wide = lax.broadcasted_iota(jnp.int32, (Z, Z), 1)
    deep = lax.broadcasted_iota(jnp.int32, (Z, Z), 0)
    beside = (deep == wide - 1) | (deep == wide + 1) | ((deep == wide) & ((wide == 0) | (wide == Z - 1)))
    edge = jnp.maximum(deep, wide)
    crossing = (deep != wide) & (lax.rem(edge, B) == 0)
    base_matrix = jnp.where(beside & jnp.logical_not(crossing), 1.0, 0.0)
    crossings = [jnp.where(beside & crossing & (edge == k * B), 1.0, 0.0) for k in range(1, K)]
    for s in range(S):
        matrix = base_matrix
        for k in range(1, K):
            matrix = matrix + jnp.where((matches[k] & (1 << s)) > 0, crossings[k - 1], 0.0)
        matrix = matrix.astype(jnp.bfloat16)
        couple[s, pl.ds(0, Z), :] = matrix
        couple[s, pl.ds(Z, Z), :] = matrix

    zero = jnp.zeros((8, Z), jnp.float32)

    def clear(x, carry):
        for s in range(S):
            for g in (g0, g1):
                g[s, x, pl.ds(0, 8), :] = zero
                g[s, x, pl.ds(YP - 8, 8), :] = zero
        return carry

    lax.fori_loop(0, XP, clear, 0)
    for s in range(S):
        for g in (g0, g1):
            for x in (0, XP - 1):
                for j in range(4):
                    g[s, x, pl.ds(8 + 8 * j, 8), :] = zero
    wide_group = lax.broadcasted_iota(jnp.int32, (16, Z), 1) // B
    scale = [
        jnp.where(jnp.broadcast_to(code[1, pl.ds(s, 1), :], (16, Z)) > 0, ROOT, 0.0) for s in range(S)
    ]

    def keep_split(s, row, value):
        high = value.astype(jnp.bfloat16)
        split[s, pl.ds(row, 16), pl.ds(0, Z)] = high
        split[s, pl.ds(row, 16), pl.ds(Z, Z)] = (value - high.astype(jnp.float32)).astype(jnp.bfloat16)

    def place_field(x, carry):
        values = []
        for s in range(S):
            for j in range(0, 4, 2):
                rows = pl.ds(8 * j, 16)
                value = raw[s, x, rows, :]
                for k in range(1, K):
                    value = jnp.where(wide_group == k, raw[orders[k][s], x, rows, :], value)
                values.append(value * scale[s])
        for s in range(S):
            for j in range(0, 4, 2):
                value = values[2 * s + j // 2]
                g0[s, x + 1, pl.ds(8 + 8 * j, 16), :] = value
                keep_split(s, pl.multiple_of(x * B, B) + 8 * j, value)
        return carry

    lax.fori_loop(0, B, place_field, 0)

    def sweep(g, i, use):
        rows = pl.ds(pl.multiple_of(i * CHUNK * B, CHUNK * B), CHUNK * B)
        depth = [
            lax.dot_general(
                split[s, rows, :], couple[s], (((1,), (0,)), ((), ())), preferred_element_type=jnp.float32
            )
            for s in range(S)
        ]
        for part in range(CHUNK):
            x = i * CHUNK + part + 1
            for j in range(4):
                row = 8 + 8 * j
                own = [g[s, x, pl.ds(row, 8), :] for s in range(S)]
                squares = own[0] * own[0]
                for s in range(1, S):
                    squares = squares + own[s] * own[s]
                sums = []
                for s in range(S):
                    total = g[s, x - 1, pl.ds(row, 8), :] + g[s, x + 1, pl.ds(row, 8), :]
                    total = total + (g[s, x, pl.ds(row - 1, 8), :] + g[s, x, pl.ds(row + 1, 8), :])
                    sums.append(total + depth[s][part * B + 8 * j : part * B + 8 * j + 8])
                use(x, j, own, squares, sums)

    def first(x, j, own, squares, sums):
        level = (1.0 - 6.0 * GRADIENT) - MIX * squares
        for s in range(S):
            change = own[s] * (level + own[s] * own[s]) + sums[s]
            g1[s, x, pl.ds(8 + 8 * j, 8), :] = own[s] + mm[s] * change

    def first_sweep(i, carry):
        sweep(g0, i, first)
        return carry

    lax.fori_loop(0, B // CHUNK, first_sweep, 0)

    own_now = code[1]
    for f in range(4):
        finish(2, f)
        for step in range(2):
            index = jnp.zeros((8, Z), jnp.int32)
            value = jnp.zeros((8, Z), jnp.float32)
            for s in range(S):
                other = jnp.broadcast_to(code_in[f, step, pl.ds(s, 1), :], (8, Z))
                same = (other == own_now) & (own_now > 0)
                index = jnp.where(same, s, index)
                value = jnp.where(same, (ROOT, 1.0)[step] * mob[...], value)
            move[step, f] = index
            weight[step, f] = value

    def add_faces(base, stride_s, stride_x, first_x, first_y, step, f):
        finish(step, f)
        flat = base.reshape(S * stride_s, Z)
        source = face_in.at[step, f].reshape(S * B, Z)
        turn, gain = move[step, f], weight[step, f]

        def eight(n, carry):
            places, values = [], []
            for i in range(8):
                cell = 8 * n + i
                got = jnp.take_along_axis(source[pl.ds(cell, 8, stride=B), :], turn, axis=0)
                if f < 2:
                    row = (first_x + (0, B - 1)[f]) * stride_x + first_y + cell
                else:
                    row = (first_x + cell) * stride_x + first_y + (0, B - 1)[f - 2]
                at = (pl.ds(row, 8, stride=stride_s), slice(None))
                places.append(at)
                values.append(flat[at] + gain * got)
            for at, value in zip(places, values):
                flat[at] = value
            return carry

        lax.fori_loop(0, B // 8, eight, 0)

    for f in range(4):
        add_faces(g1, PLANE, YP, 1, 8, 0, f)

    everyone = pltpu.make_async_remote_copy(
        send.at[pl.ds(0, nd - 1)], recv.at[pl.ds(0, nd - 1)], heat_send, heat_recv,
        device_id=(tx, ty), device_id_type=MESH,
    )
    everyone.wait_send()
    everyone.wait_recv()
    locator = jnp.broadcast_to(locator_ref[...], (Z, Z))
    order = jnp.where(locator == lax.broadcasted_iota(jnp.int32, (Z, Z), 0), 1.0, 0.0).astype(jnp.bfloat16)
    flat_recv = recv.reshape(nd * 8, Z)
    for s in range(8):
        value = (UNDERCOOL / ROOT) * (1.0 - flat_recv[pl.ds(s, nd, stride=8), :])
        value = jnp.transpose(value)
        high = value.astype(jnp.bfloat16)
        low = (value - high.astype(jnp.float32)).astype(jnp.bfloat16)
        dims = (((1,), (1,)), ((), ()))
        placed = lax.dot_general(high, order, dims, preferred_element_type=jnp.float32)
        placed = placed + lax.dot_general(low, order, dims, preferred_element_type=jnp.float32)
        for a in range(4):
            u_ref[pl.ds((8 * a + s) * B, B), :] = placed[a * B : (a + 1) * B]

    flat0, flat1 = g0.reshape(S * PLANE, Z), g1.reshape(S * PLANE, Z)

    def heat_row(side, row):
        def one(n, carry):
            u = u_ref[pl.ds(n * 8 * B + row, 8, stride=B), :]
            values = []
            for s in range(S):
                at = (pl.ds(s * PLANE + (n * 8 + 1) * YP + 8 + row, 8, stride=YP), slice(None))
                own = flat0[at]
                values.append(flat1[at] + (mm[s] * u) * (own * (ROOT - own)))
            for s in range(S):
                face_y[1, side, s, pl.ds(pl.multiple_of(n * 8, 8), 8), :] = values[s]
            return carry

        lax.fori_loop(0, B // 8, one, 0)

    def heat_term(x):
        for j in (0, 2):
            u = u_ref[pl.ds((x - 1) * B + 8 * j, 16), :]
            values = []
            for s in range(S):
                at = (s, x, pl.ds(8 + 8 * j, 16), slice(None))
                own = g0[at]
                gain = jnp.concatenate([mm[s], mm[s]], axis=0)
                values.append(g1[at] + (gain * u) * (own * (ROOT - own)))
            for s in range(S):
                g1[s, x, pl.ds(8 + 8 * j, 16), :] = values[s]
                keep_split(s, pl.multiple_of((x - 1) * B, B) + 8 * j, values[s])

    heat_row(0, 0)
    begin(1, 2)
    heat_row(1, B - 1)
    begin(1, 3)
    heat_term(1)
    begin(1, 0)
    heat_term(B)
    begin(1, 1)

    def heat_rest(x, carry):
        heat_term(x)
        return carry

    lax.fori_loop(2, B, heat_rest, 0)

    def second(x, j, own, squares, sums):
        u = u_ref[pl.ds((x - 1) * B + 8 * j, 8), :]
        level = (1.0 - 6.0 * GRADIENT) + ROOT * u - MIX * squares
        for s in range(S):
            change = own[s] * (level + own[s] * (own[s] - u)) + sums[s]
            out[s, x - 1, pl.ds(8 * j, 8), :] = own[s] + mm[s] * change

    def second_sweep(i, carry):
        sweep(g1, i, second)
        return carry

    lax.fori_loop(0, B // CHUNK, second_sweep, 0)
    for f in range(4):
        add_faces(out, B * B, B, 0, 0, 1, f)


def restore(order, moved, result_hbm, result, out_sem):
    group = lax.broadcasted_iota(jnp.int32, (8, Z), 1) // B
    places = [[order[k, s] for s in range(S)] for k in range(K)]

    def piece(i):
        planes = pl.ds(i * PIECE, PIECE)
        return pltpu.make_async_copy(result.at[:, planes], result_hbm.at[:, planes], out_sem)

    def plane(x):
        values = []
        for s in range(S):
            for j in range(4):
                rows = pl.ds(8 * j, 8)
                value = moved[s, x, rows, :]
                for k in range(1, K):
                    value = jnp.where(group == k, moved[places[k][s], x, rows, :], value)
                values.append(value * (1.0 / ROOT))
        for s in range(S):
            for j in range(4):
                result[s, x, pl.ds(8 * j, 8), :] = values[4 * s + j]

    def one(i, carry):
        for x in range(PIECE):
            plane(i * PIECE + x)
        piece(i).start()
        return carry

    lax.fori_loop(0, B // PIECE, one, 0)
    pltpu.make_async_copy(result, result_hbm, out_sem).wait()


def on_device(ntx, nty, field, heat, label, count, speed, locator):
    nd = ntx * nty
    in_hbm = pl.BlockSpec(memory_space=pltpu.HBM)
    f32, i32 = jnp.float32, jnp.int32
    moved, order = pl.pallas_call(
        functools.partial(kernel, ntx, nty),
        out_shape=(pltpu.VMEM(field.shape, f32), pltpu.SMEM((K, S), i32)),
        in_specs=[in_hbm] * 6,
        out_specs=(pl.BlockSpec(memory_space=pltpu.VMEM), pl.BlockSpec(memory_space=pltpu.SMEM)),
        scratch_shapes=[
            pltpu.VMEM((S, B, B, Z), f32),
            pltpu.VMEM((S, XP, YP, Z), f32),
            pltpu.VMEM((S, XP, YP, Z), f32),
            pltpu.VMEM(heat.shape[1:], f32),
            pltpu.VMEM((nd, 8, Z), f32),
            pltpu.VMEM((nd, 8, Z), f32),
            pltpu.VMEM((B * B, Z), f32),
            pltpu.VMEM((S, B * B, 2 * Z), jnp.bfloat16),
            pltpu.VMEM((S, 2 * Z, Z), jnp.bfloat16),
            pltpu.SMEM(label.shape, i32),
            pltpu.SMEM(count.shape, i32),
            pltpu.SMEM(speed.shape, f32),
            pltpu.VMEM((1, Z), i32),
            pltpu.VMEM((2, 8, Z), i32),
            pltpu.VMEM((4, 2, 8, Z), i32),
            pltpu.VMEM((2, 2, S, B, Z), f32),
            pltpu.VMEM((2, 4, S, B, Z), f32),
            pltpu.VMEM((2, 4, 8, Z), i32),
            pltpu.VMEM((2, 4, 8, Z), f32),
            pltpu.VMEM((8, Z), f32),
            pltpu.VMEM((S, 8, Z), f32),
            pltpu.SemaphoreType.DMA((6,)),
            pltpu.SemaphoreType.DMA,
            pltpu.SemaphoreType.DMA,
            pltpu.SemaphoreType.DMA((12,)),
            pltpu.SemaphoreType.DMA((12,)),
            pltpu.SemaphoreType.DMA((12,)),
        ],
        compiler_params=pltpu.CompilerParams(
            collective_id=0, has_side_effects=True, vmem_limit_bytes=59 * 2**20
        ),
        name="grains",
    )(field, heat, label, count, speed, locator.reshape(1, Z))
    return pl.pallas_call(
        restore,
        out_shape=jax.ShapeDtypeStruct(field.shape, f32),
        in_specs=[pl.BlockSpec(memory_space=pltpu.SMEM), pl.BlockSpec(memory_space=pltpu.VMEM)],
        out_specs=in_hbm,
        scratch_shapes=[
            pltpu.VMEM(field.shape, f32),
            pltpu.SemaphoreType.DMA,
        ],
        compiler_params=pltpu.CompilerParams(vmem_limit_bytes=32 * 2**20),
        name="restore",
    )(order, moved)


def solution(mesh):
    ntx, nty = mesh.shape["track"], mesh.shape["cross"]
    return jax.shard_map(
        functools.partial(on_device, ntx, nty),
        mesh=mesh,
        in_specs=(
            P(None, "track", "cross", None),
            P(("track", "cross"), None, None),
            P("track", "cross", None, None),
            P("track", "cross", None),
            P(),
            P(),
        ),
        out_specs=P(None, "track", "cross", None),
        check_vma=False,
    )
```

```python
import functools
import math

import jax
import jax.numpy as jnp
from jax import lax
from jax.experimental import pallas as pl
from jax.experimental.pallas import tpu as pltpu
from jax.sharding import PartitionSpec as P

MIX = 1.5
GRADIENT = 1.0
UNDERCOOL = 4.0
DT = 0.06
ROOT = math.sqrt(2.0)
MESH = pl.DeviceIdType.MESH

S = 8
B = 32
K = 4
Z = B * K
XP = B + 2
YP = B + 16
PLANE = XP * YP
PIECE = 2
CHUNK = 8


def iota(dim):
    return lax.broadcasted_iota(jnp.int32, (8, Z), dim)


def kernel(
    ntx, nty,
    field_hbm, slab_hbm, label_hbm, count_hbm, speed_hbm, locator_hbm,
    out, order_out,
    raw, g0, g1, slab, send, recv, u_ref, split, couple,
    label, count, speed, locator_ref,
    code, code_in, face_y, face_in,
    move, weight, mob, mm,
    all_in, load_sem, heat_send, heat_recv, send_sem, recv_sem, own_sem,
):
    nd = ntx * nty
    tx, ty = lax.axis_index("track"), lax.axis_index("cross")
    me = tx * nty + ty
    lane, sub = iota(1), iota(0)

    def load(source, target, index):
        return pltpu.make_async_copy(source, target, load_sem.at[index])

    loads = (
        load(slab_hbm.at[0], slab, 0),
        load(field_hbm, raw, 1),
        load(label_hbm, label, 2),
        load(count_hbm, count, 3),
        load(speed_hbm, speed, 4),
        load(locator_hbm, locator_ref, 5),
    )
    loads[0].start()
    barrier = pltpu.get_barrier_semaphore()

    def tell(axis, semaphore_at):
        def one(i, carry):
            px = lax.rem(tx + i, ntx) if axis == 0 else tx
            py = lax.rem(ty + i, nty) if axis == 1 else ty
            pl.semaphore_signal(semaphore_at(i), inc=1, device_id=(px, py), device_id_type=MESH)
            return carry

        lax.fori_loop(1, (ntx, nty)[axis], one, 0)

    tell(1, lambda i: barrier)
    tell(0, lambda i: barrier)
    for entry in loads[1:]:
        entry.start()

    loads[0].wait()
    group = lane // B

    def patches(px, carry):
        for half in range(nty * B // Z):
            rows = [slab[pl.ds(px * B + 8 * a, 8), pl.ds(half * Z, Z)] for a in range(4)]
            for q in range(4):
                tile = rows[q] if q == 0 else None
                parts = [rows[a] if a == q else pltpu.roll(rows[a], (B * (a - q)) % Z, axis=1) for a in range(4)]
                tile = parts[0]
                for a in range(1, 4):
                    tile = jnp.where(group == a, parts[a], tile)
                send[px * nty + half * 4 + q] = tile
        return carry

    lax.fori_loop(0, ntx, patches, 0)
    recv[me] = send[me]

    lower_x, upper_x = jnp.maximum(tx - 1, 0), jnp.minimum(tx + 1, ntx - 1)
    lower_y, upper_y = jnp.maximum(ty - 1, 0), jnp.minimum(ty + 1, nty - 1)
    at_end = (tx == 0, tx == ntx - 1, ty == 0, ty == nty - 1)
    target = ((lower_x, ty), (upper_x, ty), (tx, lower_y), (tx, upper_y))

    def face(step, f):
        if f >= 2:
            return face_y.at[step, f - 2]
        if step == 0:
            return field_hbm.at[:, (0, B - 1)[f]]
        return g1.at[:, (1, B)[f], pl.ds(8, B), :]

    def to_peer(step, f):
        if step == 2:
            source, here, there = code, code_in.at[f], code_in.at[f ^ 1]
        else:
            source, here, there = face(step, f), face_in.at[step, f], face_in.at[step, f ^ 1]
        sem = step * 4 + f
        remote = functools.partial(
            pltpu.make_async_remote_copy,
            source, there, send_sem.at[sem], recv_sem.at[sem ^ 1], device_id=target[f], device_id_type=MESH,
        )
        local = functools.partial(pltpu.make_async_copy, source, here, own_sem.at[sem])
        return remote, local

    def begin(step, f):
        remote, local = to_peer(step, f)

        @pl.when(jnp.logical_not(at_end[f]))
        def _():
            remote().start()

        @pl.when(at_end[f])
        def _():
            local().start()

    def finish(step, f):
        remote, local = to_peer(step, f)
        back, _ = to_peer(step, f ^ 1)

        @pl.when(jnp.logical_not(at_end[f]))
        def _():
            remote().wait_send()
            back().wait_recv()

        @pl.when(at_end[f])
        def _():
            local().wait()

    loads[1].wait()
    flat_raw = raw.reshape(S * B * B, Z)

    def pack_raw(s, carry):
        for side, row in ((0, 0), (1, B - 1)):
            values = [flat_raw[pl.ds((s * B + x) * B + row, 8, stride=B), :] for x in range(0, B, 8)]
            for x in range(0, B, 8):
                face_y[0, side, s, pl.ds(x, 8), :] = values[x // 8]
        return carry

    lax.fori_loop(0, S, pack_raw, 0)
    pl.semaphore_wait(barrier, ntx + nty - 2)
    tell(1, lambda i: all_in.at[i])

    def to_row(py, first):
        def one(i, carry):
            px = lax.rem(tx + i, ntx)
            pltpu.make_async_remote_copy(
                send.at[px * nty + py], recv.at[me], heat_send, heat_recv, device_id=(px, py), device_id_type=MESH
            ).start()
            return carry

        lax.fori_loop(first, ntx, one, 0)

    def next_row(i, carry):
        pl.semaphore_wait(all_in.at[i], 1)
        to_row(lax.rem(ty + nty - i, nty), 0)
        return carry

    to_row(ty, 1)
    begin(0, 2)
    begin(0, 3)
    begin(0, 0)
    begin(0, 1)
    lax.fori_loop(1, nty, next_row, 0)

    loads[2].wait()
    loads[3].wait()
    loads[4].wait()
    loads[5].wait()
    lives, codes, orders, matches = [], [], [], []
    for k in range(K):
        live = [jnp.where(s < count[0, 0, k], label[0, 0, k, s] + 1, 0) for s in range(S)]
        if k == 0:
            order, code_at, matched = [jnp.int32(s) for s in range(S)], live, None
        else:
            bits = []
            for j in range(S):
                bit = jnp.int32(0)
                for p in range(S):
                    bit = jnp.where((live[j] == codes[k - 1][p]) & (live[j] > 0), 1 << p, bit)
                bits.append(bit)
            matched = functools.reduce(jnp.bitwise_or, bits)
            free = matched ^ (2**S - 1)
            for j in range(S):
                low = free & -free
                free = jnp.where(bits[j] == 0, free ^ low, free)
                bits[j] = jnp.where(bits[j] == 0, low, bits[j])
            order, code_at = [], []
            for p in range(S):
                slot, here = jnp.int32(0), live[0]
                for j in range(1, S):
                    slot = jnp.where(bits[j] == 1 << p, j, slot)
                    here = jnp.where(bits[j] == 1 << p, live[j], here)
                order.append(slot)
                code_at.append(here)
            for j in range(S):
                place = jnp.int32(0)
                for p in range(1, S):
                    place = jnp.where(bits[j] == 1 << p, p, place)
                order_out[k, j] = place
        if k == 0:
            for j in range(S):
                order_out[k, j] = j
        lives.append(live)
        codes.append(code_at)
        orders.append(order)
        matches.append(matched)
    own_code = jnp.zeros((8, Z), jnp.int32)
    listed = jnp.zeros((8, Z), jnp.int32)
    mobility = jnp.zeros((8, Z), jnp.float32)
    for k in range(K):
        for s in range(S):
            here = (sub == s) & (group == k)
            own_code = jnp.where(here, codes[k][s], own_code)
            listed = jnp.where(here, lives[k][s], listed)
            mobility = jnp.where(here, speed[label[0, 0, k, orders[k][s]]], mobility)
    code[0] = listed
    code[1] = own_code
    for f in range(4):
        begin(2, f)
    mob[...] = DT * mobility
    for s in range(S):
        mm[s] = jnp.broadcast_to(mob[pl.ds(s, 1), :], (8, Z))

    wide = lax.broadcasted_iota(jnp.int32, (Z, Z), 1)
    deep = lax.broadcasted_iota(jnp.int32, (Z, Z), 0)
    beside = (deep == wide - 1) | (deep == wide + 1) | ((deep == wide) & ((wide == 0) | (wide == Z - 1)))
    edge = jnp.maximum(deep, wide)
    crossing = (deep != wide) & (lax.rem(edge, B) == 0)
    base_matrix = jnp.where(beside & jnp.logical_not(crossing), 1.0, 0.0)
    crossings = [jnp.where(beside & crossing & (edge == k * B), 1.0, 0.0) for k in range(1, K)]
    for s in range(S):
        matrix = base_matrix
        for k in range(1, K):
            matrix = matrix + jnp.where((matches[k] & (1 << s)) > 0, crossings[k - 1], 0.0)
        matrix = matrix.astype(jnp.bfloat16)
        couple[s, pl.ds(0, Z), :] = matrix
        couple[s, pl.ds(Z, Z), :] = matrix

    zero = jnp.zeros((8, Z), jnp.float32)

    def clear(x, carry):
        for s in range(S):
            for g in (g0, g1):
                g[s, x, pl.ds(0, 8), :] = zero
                g[s, x, pl.ds(YP - 8, 8), :] = zero
        return carry

    lax.fori_loop(0, XP, clear, 0)
    for s in range(S):
        for g in (g0, g1):
            for x in (0, XP - 1):
                for j in range(4):
                    g[s, x, pl.ds(8 + 8 * j, 8), :] = zero
    wide_group = lax.broadcasted_iota(jnp.int32, (16, Z), 1) // B
    scale = [
        jnp.where(jnp.broadcast_to(code[1, pl.ds(s, 1), :], (16, Z)) > 0, ROOT, 0.0) for s in range(S)
    ]

    def keep_split(s, row, value):
        high = value.astype(jnp.bfloat16)
        split[s, pl.ds(row, 16), pl.ds(0, Z)] = high
        split[s, pl.ds(row, 16), pl.ds(Z, Z)] = (value - high.astype(jnp.float32)).astype(jnp.bfloat16)

    def place_field(x, carry):
        values = []
        for s in range(S):
            for j in range(0, 4, 2):
                rows = pl.ds(8 * j, 16)
                value = raw[s, x, rows, :]
                for k in range(1, K):
                    value = jnp.where(wide_group == k, raw[orders[k][s], x, rows, :], value)
                values.append(value * scale[s])
        for s in range(S):
            for j in range(0, 4, 2):
                value = values[2 * s + j // 2]
                g0[s, x + 1, pl.ds(8 + 8 * j, 16), :] = value
                keep_split(s, pl.multiple_of(x * B, B) + 8 * j, value)
        return carry

    lax.fori_loop(0, B, place_field, 0)

    def sweep(g, i, use):
        rows = pl.ds(pl.multiple_of(i * CHUNK * B, CHUNK * B), CHUNK * B)
        depth = [
            lax.dot_general(
                split[s, rows, :], couple[s], (((1,), (0,)), ((), ())), preferred_element_type=jnp.float32
            )
            for s in range(S)
        ]
        for part in range(CHUNK):
            x = i * CHUNK + part + 1
            for j in range(4):
                row = 8 + 8 * j
                own = [g[s, x, pl.ds(row, 8), :] for s in range(S)]
                squares = own[0] * own[0]
                for s in range(1, S):
                    squares = squares + own[s] * own[s]
                sums = []
                for s in range(S):
                    total = g[s, x - 1, pl.ds(row, 8), :] + g[s, x + 1, pl.ds(row, 8), :]
                    total = total + (g[s, x, pl.ds(row - 1, 8), :] + g[s, x, pl.ds(row + 1, 8), :])
                    sums.append(total + depth[s][part * B + 8 * j : part * B + 8 * j + 8])
                use(x, j, own, squares, sums)

    def first(x, j, own, squares, sums):
        level = (1.0 - 6.0 * GRADIENT) - MIX * squares
        for s in range(S):
            change = own[s] * (level + own[s] * own[s]) + sums[s]
            g1[s, x, pl.ds(8 + 8 * j, 8), :] = own[s] + mm[s] * change

    def first_sweep(i, carry):
        sweep(g0, i, first)
        return carry

    lax.fori_loop(0, B // CHUNK, first_sweep, 0)

    own_now = code[1]
    for f in range(4):
        finish(2, f)
        for step in range(2):
            index = jnp.zeros((8, Z), jnp.int32)
            value = jnp.zeros((8, Z), jnp.float32)
            for s in range(S):
                other = jnp.broadcast_to(code_in[f, step, pl.ds(s, 1), :], (8, Z))
                same = (other == own_now) & (own_now > 0)
                index = jnp.where(same, s, index)
                value = jnp.where(same, (ROOT, 1.0)[step] * mob[...], value)
            move[step, f] = index
            weight[step, f] = value

    def add_faces(base, stride_s, stride_x, first_x, first_y, step, f):
        finish(step, f)
        flat = base.reshape(S * stride_s, Z)
        source = face_in.at[step, f].reshape(S * B, Z)
        turn, gain = move[step, f], weight[step, f]

        def eight(n, carry):
            places, values = [], []
            for i in range(8):
                cell = 8 * n + i
                got = jnp.take_along_axis(source[pl.ds(cell, 8, stride=B), :], turn, axis=0)
                if f < 2:
                    row = (first_x + (0, B - 1)[f]) * stride_x + first_y + cell
                else:
                    row = (first_x + cell) * stride_x + first_y + (0, B - 1)[f - 2]
                at = (pl.ds(row, 8, stride=stride_s), slice(None))
                places.append(at)
                values.append(flat[at] + gain * got)
            for at, value in zip(places, values):
                flat[at] = value
            return carry

        lax.fori_loop(0, B // 8, eight, 0)

    for f in range(4):
        add_faces(g1, PLANE, YP, 1, 8, 0, f)

    everyone = pltpu.make_async_remote_copy(
        send.at[pl.ds(0, nd - 1)], recv.at[pl.ds(0, nd - 1)], heat_send, heat_recv,
        device_id=(tx, ty), device_id_type=MESH,
    )
    everyone.wait_send()
    everyone.wait_recv()
    locator = jnp.broadcast_to(locator_ref[...], (Z, Z))
    order = jnp.where(locator == lax.broadcasted_iota(jnp.int32, (Z, Z), 0), 1.0, 0.0).astype(jnp.bfloat16)
    flat_recv = recv.reshape(nd * 8, Z)
    for s in range(8):
        value = (UNDERCOOL / ROOT) * (1.0 - flat_recv[pl.ds(s, nd, stride=8), :])
        value = jnp.transpose(value)
        high = value.astype(jnp.bfloat16)
        low = (value - high.astype(jnp.float32)).astype(jnp.bfloat16)
        dims = (((1,), (1,)), ((), ()))
        placed = lax.dot_general(high, order, dims, preferred_element_type=jnp.float32)
        placed = placed + lax.dot_general(low, order, dims, preferred_element_type=jnp.float32)
        for a in range(4):
            u_ref[pl.ds((8 * a + s) * B, B), :] = placed[a * B : (a + 1) * B]

    flat0, flat1 = g0.reshape(S * PLANE, Z), g1.reshape(S * PLANE, Z)

    def heat_row(side, row):
        def one(n, carry):
            u = u_ref[pl.ds(n * 8 * B + row, 8, stride=B), :]
            values = []
            for s in range(S):
                at = (pl.ds(s * PLANE + (n * 8 + 1) * YP + 8 + row, 8, stride=YP), slice(None))
                own = flat0[at]
                values.append(flat1[at] + (mm[s] * u) * (own * (ROOT - own)))
            for s in range(S):
                face_y[1, side, s, pl.ds(pl.multiple_of(n * 8, 8), 8), :] = values[s]
            return carry

        lax.fori_loop(0, B // 8, one, 0)

    def heat_term(x):
        for j in (0, 2):
            u = u_ref[pl.ds((x - 1) * B + 8 * j, 16), :]
            values = []
            for s in range(S):
                at = (s, x, pl.ds(8 + 8 * j, 16), slice(None))
                own = g0[at]
                gain = jnp.concatenate([mm[s], mm[s]], axis=0)
                values.append(g1[at] + (gain * u) * (own * (ROOT - own)))
            for s in range(S):
                g1[s, x, pl.ds(8 + 8 * j, 16), :] = values[s]
                keep_split(s, pl.multiple_of((x - 1) * B, B) + 8 * j, values[s])

    heat_row(0, 0)
    begin(1, 2)
    heat_row(1, B - 1)
    begin(1, 3)
    heat_term(1)
    begin(1, 0)
    heat_term(B)
    begin(1, 1)

    def heat_rest(x, carry):
        heat_term(x)
        return carry

    lax.fori_loop(2, B, heat_rest, 0)

    def second(x, j, own, squares, sums):
        u = u_ref[pl.ds((x - 1) * B + 8 * j, 8), :]
        level = (1.0 - 6.0 * GRADIENT) + ROOT * u - MIX * squares
        for s in range(S):
            change = own[s] * (level + own[s] * (own[s] - u)) + sums[s]
            out[s, x - 1, pl.ds(8 * j, 8), :] = own[s] + mm[s] * change

    def second_sweep(i, carry):
        sweep(g1, i, second)
        return carry

    lax.fori_loop(0, B // CHUNK, second_sweep, 0)
    for f in range(4):
        add_faces(out, B * B, B, 0, 0, 1, f)


def restore(order, moved, result_hbm, result, out_sem):
    group = lax.broadcasted_iota(jnp.int32, (8, Z), 1) // B
    places = [[order[k, s] for s in range(S)] for k in range(K)]

    def piece(i):
        planes = pl.ds(i * PIECE, PIECE)
        return pltpu.make_async_copy(result.at[:, planes], result_hbm.at[:, planes], out_sem)

    def plane(x):
        values = []
        for s in range(S):
            for j in range(4):
                rows = pl.ds(8 * j, 8)
                value = moved[s, x, rows, :]
                for k in range(1, K):
                    value = jnp.where(group == k, moved[places[k][s], x, rows, :], value)
                values.append(value * (1.0 / ROOT))
        for s in range(S):
            for j in range(4):
                result[s, x, pl.ds(8 * j, 8), :] = values[4 * s + j]

    def one(i, carry):
        for x in range(PIECE):
            plane(i * PIECE + x)
        piece(i).start()
        return carry

    lax.fori_loop(0, B // PIECE, one, 0)
    pltpu.make_async_copy(result, result_hbm, out_sem).wait()


def on_device(ntx, nty, field, heat, label, count, speed, locator):
    nd = ntx * nty
    in_hbm = pl.BlockSpec(memory_space=pltpu.HBM)
    f32, i32 = jnp.float32, jnp.int32
    moved, order = pl.pallas_call(
        functools.partial(kernel, ntx, nty),
        out_shape=(pltpu.VMEM(field.shape, f32), pltpu.SMEM((K, S), i32)),
        in_specs=[in_hbm] * 6,
        out_specs=(pl.BlockSpec(memory_space=pltpu.VMEM), pl.BlockSpec(memory_space=pltpu.SMEM)),
        scratch_shapes=[
            pltpu.VMEM((S, B, B, Z), f32),
            pltpu.VMEM((S, XP, YP, Z), f32),
            pltpu.VMEM((S, XP, YP, Z), f32),
            pltpu.VMEM(heat.shape[1:], f32),
            pltpu.VMEM((nd, 8, Z), f32),
            pltpu.VMEM((nd, 8, Z), f32),
            pltpu.VMEM((B * B, Z), f32),
            pltpu.VMEM((S, B * B, 2 * Z), jnp.bfloat16),
            pltpu.VMEM((S, 2 * Z, Z), jnp.bfloat16),
            pltpu.SMEM(label.shape, i32),
            pltpu.SMEM(count.shape, i32),
            pltpu.SMEM(speed.shape, f32),
            pltpu.VMEM((1, Z), i32),
            pltpu.VMEM((2, 8, Z), i32),
            pltpu.VMEM((4, 2, 8, Z), i32),
            pltpu.VMEM((2, 2, S, B, Z), f32),
            pltpu.VMEM((2, 4, S, B, Z), f32),
            pltpu.VMEM((2, 4, 8, Z), i32),
            pltpu.VMEM((2, 4, 8, Z), f32),
            pltpu.VMEM((8, Z), f32),
            pltpu.VMEM((S, 8, Z), f32),
            pltpu.SemaphoreType.REGULAR((nty,)),
            pltpu.SemaphoreType.DMA((6,)),
            pltpu.SemaphoreType.DMA,
            pltpu.SemaphoreType.DMA,
            pltpu.SemaphoreType.DMA((12,)),
            pltpu.SemaphoreType.DMA((12,)),
            pltpu.SemaphoreType.DMA((12,)),
        ],
        compiler_params=pltpu.CompilerParams(
            collective_id=0, has_side_effects=True, vmem_limit_bytes=59 * 2**20
        ),
        name="grains",
    )(field, heat, label, count, speed, locator.reshape(1, Z))
    return pl.pallas_call(
        restore,
        out_shape=jax.ShapeDtypeStruct(field.shape, f32),
        in_specs=[pl.BlockSpec(memory_space=pltpu.SMEM), pl.BlockSpec(memory_space=pltpu.VMEM)],
        out_specs=in_hbm,
        scratch_shapes=[
            pltpu.VMEM(field.shape, f32),
            pltpu.SemaphoreType.DMA,
        ],
        compiler_params=pltpu.CompilerParams(vmem_limit_bytes=32 * 2**20),
        name="restore",
    )(order, moved)


def solution(mesh):
    ntx, nty = mesh.shape["track"], mesh.shape["cross"]
    return jax.shard_map(
        functools.partial(on_device, ntx, nty),
        mesh=mesh,
        in_specs=(
            P(None, "track", "cross", None),
            P(("track", "cross"), None, None),
            P("track", "cross", None, None),
            P("track", "cross", None),
            P(),
            P(),
        ),
        out_specs=P(None, "track", "cross", None),
        check_vma=False,
    )
```

```python
import functools
import math

import jax
import jax.numpy as jnp
from jax import lax
from jax.experimental import pallas as pl
from jax.experimental.pallas import tpu as pltpu
from jax.sharding import PartitionSpec as P

MIX = 1.5
GRADIENT = 1.0
UNDERCOOL = 4.0
DT = 0.06
ROOT = math.sqrt(2.0)
MESH = pl.DeviceIdType.MESH

S = 8
B = 32
K = 4
Z = B * K
XP = B + 2
YP = B + 16
PLANE = XP * YP
PIECE = 4
CHUNK = 8


def iota(dim):
    return lax.broadcasted_iota(jnp.int32, (8, Z), dim)


def kernel(
    ntx, nty,
    field_hbm, slab_hbm, label_hbm, count_hbm, speed_hbm, locator_hbm,
    out, order_out,
    raw, g0, g1, slab, send, recv, u_ref, split, couple,
    label, count, speed, locator_ref,
    code, code_in, face_y, face_in,
    move, weight, mob, mm,
    all_in, load_sem, heat_send, heat_recv, send_sem, recv_sem, own_sem,
):
    nd = ntx * nty
    tx, ty = lax.axis_index("track"), lax.axis_index("cross")
    me = tx * nty + ty
    lane, sub = iota(1), iota(0)

    def load(source, target, index):
        return pltpu.make_async_copy(source, target, load_sem.at[index])

    loads = (
        load(slab_hbm.at[0], slab, 0),
        load(field_hbm, raw, 1),
        load(label_hbm, label, 2),
        load(count_hbm, count, 3),
        load(speed_hbm, speed, 4),
        load(locator_hbm, locator_ref, 5),
    )
    loads[0].start()
    barrier = pltpu.get_barrier_semaphore()

    def tell(axis, semaphore_at):
        def one(i, carry):
            px = lax.rem(tx + i, ntx) if axis == 0 else tx
            py = lax.rem(ty + i, nty) if axis == 1 else ty
            pl.semaphore_signal(semaphore_at(i), inc=1, device_id=(px, py), device_id_type=MESH)
            return carry

        lax.fori_loop(1, (ntx, nty)[axis], one, 0)

    tell(1, lambda i: barrier)
    tell(0, lambda i: barrier)
    for entry in loads[1:]:
        entry.start()

    loads[0].wait()
    group = lane // B

    def patches(px, carry):
        for half in range(nty * B // Z):
            rows = [slab[pl.ds(px * B + 8 * a, 8), pl.ds(half * Z, Z)] for a in range(4)]
            for q in range(4):
                tile = rows[q] if q == 0 else None
                parts = [rows[a] if a == q else pltpu.roll(rows[a], (B * (a - q)) % Z, axis=1) for a in range(4)]
                tile = parts[0]
                for a in range(1, 4):
                    tile = jnp.where(group == a, parts[a], tile)
                send[px * nty + half * 4 + q] = tile
        return carry

    lax.fori_loop(0, ntx, patches, 0)
    recv[me] = send[me]

    lower_x, upper_x = jnp.maximum(tx - 1, 0), jnp.minimum(tx + 1, ntx - 1)
    lower_y, upper_y = jnp.maximum(ty - 1, 0), jnp.minimum(ty + 1, nty - 1)
    at_end = (tx == 0, tx == ntx - 1, ty == 0, ty == nty - 1)
    target = ((lower_x, ty), (upper_x, ty), (tx, lower_y), (tx, upper_y))

    def face(step, f):
        if f >= 2:
            return face_y.at[step, f - 2]
        if step == 0:
            return field_hbm.at[:, (0, B - 1)[f]]
        return g1.at[:, (1, B)[f], pl.ds(8, B), :]

    def to_peer(step, f):
        if step == 2:
            source, here, there = code, code_in.at[f], code_in.at[f ^ 1]
        else:
            source, here, there = face(step, f), face_in.at[step, f], face_in.at[step, f ^ 1]
        sem = step * 4 + f
        remote = functools.partial(
            pltpu.make_async_remote_copy,
            source, there, send_sem.at[sem], recv_sem.at[sem ^ 1], device_id=target[f], device_id_type=MESH,
        )
        local = functools.partial(pltpu.make_async_copy, source, here, own_sem.at[sem])
        return remote, local

    def begin(step, f):
        remote, local = to_peer(step, f)

        @pl.when(jnp.logical_not(at_end[f]))
        def _():
            remote().start()

        @pl.when(at_end[f])
        def _():
            local().start()

    def finish(step, f):
        remote, local = to_peer(step, f)
        back, _ = to_peer(step, f ^ 1)

        @pl.when(jnp.logical_not(at_end[f]))
        def _():
            remote().wait_send()
            back().wait_recv()

        @pl.when(at_end[f])
        def _():
            local().wait()

    loads[1].wait()
    flat_raw = raw.reshape(S * B * B, Z)

    def pack_raw(s, carry):
        for side, row in ((0, 0), (1, B - 1)):
            values = [flat_raw[pl.ds((s * B + x) * B + row, 8, stride=B), :] for x in range(0, B, 8)]
            for x in range(0, B, 8):
                face_y[0, side, s, pl.ds(x, 8), :] = values[x // 8]
        return carry

    lax.fori_loop(0, S, pack_raw, 0)
    pl.semaphore_wait(barrier, ntx + nty - 2)
    tell(1, lambda i: all_in.at[i])

    def to_row(py, first):
        def one(i, carry):
            px = lax.rem(tx + i, ntx)
            pltpu.make_async_remote_copy(
                send.at[px * nty + py], recv.at[me], heat_send, heat_recv, device_id=(px, py), device_id_type=MESH
            ).start()
            return carry

        lax.fori_loop(first, ntx, one, 0)

    def next_row(i, carry):
        pl.semaphore_wait(all_in.at[i], 1)
        to_row(lax.rem(ty + nty - i, nty), 0)
        return carry

    to_row(ty, 1)
    begin(0, 2)
    begin(0, 3)
    begin(0, 0)
    begin(0, 1)
    lax.fori_loop(1, nty, next_row, 0)

    loads[2].wait()
    loads[3].wait()
    loads[4].wait()
    loads[5].wait()
    lives, codes, orders, matches = [], [], [], []
    for k in range(K):
        live = [jnp.where(s < count[0, 0, k], label[0, 0, k, s] + 1, 0) for s in range(S)]
        if k == 0:
            order, code_at, matched = [jnp.int32(s) for s in range(S)], live, None
        else:
            bits = []
            for j in range(S):
                bit = jnp.int32(0)
                for p in range(S):
                    bit = jnp.where((live[j] == codes[k - 1][p]) & (live[j] > 0), 1 << p, bit)
                bits.append(bit)
            matched = functools.reduce(jnp.bitwise_or, bits)
            free = matched ^ (2**S - 1)
            for j in range(S):
                low = free & -free
                free = jnp.where(bits[j] == 0, free ^ low, free)
                bits[j] = jnp.where(bits[j] == 0, low, bits[j])
            order, code_at = [], []
            for p in range(S):
                slot, here = jnp.int32(0), live[0]
                for j in range(1, S):
                    slot = jnp.where(bits[j] == 1 << p, j, slot)
                    here = jnp.where(bits[j] == 1 << p, live[j], here)
                order.append(slot)
                code_at.append(here)
            for j in range(S):
                place = jnp.int32(0)
                for p in range(1, S):
                    place = jnp.where(bits[j] == 1 << p, p, place)
                order_out[k, j] = place
        if k == 0:
            for j in range(S):
                order_out[k, j] = j
        lives.append(live)
        codes.append(code_at)
        orders.append(order)
        matches.append(matched)
    own_code = jnp.zeros((8, Z), jnp.int32)
    listed = jnp.zeros((8, Z), jnp.int32)
    mobility = jnp.zeros((8, Z), jnp.float32)
    for k in range(K):
        for s in range(S):
            here = (sub == s) & (group == k)
            own_code = jnp.where(here, codes[k][s], own_code)
            listed = jnp.where(here, lives[k][s], listed)
            mobility = jnp.where(here, speed[label[0, 0, k, orders[k][s]]], mobility)
    code[0] = listed
    code[1] = own_code
    for f in range(4):
        begin(2, f)
    mob[...] = DT * mobility
    for s in range(S):
        mm[s] = jnp.broadcast_to(mob[pl.ds(s, 1), :], (8, Z))

    wide = lax.broadcasted_iota(jnp.int32, (Z, Z), 1)
    deep = lax.broadcasted_iota(jnp.int32, (Z, Z), 0)
    beside = (deep == wide - 1) | (deep == wide + 1) | ((deep == wide) & ((wide == 0) | (wide == Z - 1)))
    edge = jnp.maximum(deep, wide)
    crossing = (deep != wide) & (lax.rem(edge, B) == 0)
    base_matrix = jnp.where(beside & jnp.logical_not(crossing), 1.0, 0.0)
    crossings = [jnp.where(beside & crossing & (edge == k * B), 1.0, 0.0) for k in range(1, K)]
    for s in range(S):
        matrix = base_matrix
        for k in range(1, K):
            matrix = matrix + jnp.where((matches[k] & (1 << s)) > 0, crossings[k - 1], 0.0)
        matrix = matrix.astype(jnp.bfloat16)
        couple[s, pl.ds(0, Z), :] = matrix
        couple[s, pl.ds(Z, Z), :] = matrix

    zero = jnp.zeros((8, Z), jnp.float32)

    def clear(x, carry):
        for s in range(S):
            for g in (g0, g1):
                g[s, x, pl.ds(0, 8), :] = zero
                g[s, x, pl.ds(YP - 8, 8), :] = zero
        return carry

    lax.fori_loop(0, XP, clear, 0)
    for s in range(S):
        for g in (g0, g1):
            for x in (0, XP - 1):
                for j in range(4):
                    g[s, x, pl.ds(8 + 8 * j, 8), :] = zero
    wide_group = lax.broadcasted_iota(jnp.int32, (16, Z), 1) // B
    scale = [
        jnp.where(jnp.broadcast_to(code[1, pl.ds(s, 1), :], (16, Z)) > 0, ROOT, 0.0) for s in range(S)
    ]

    def keep_split(s, row, value):
        high = value.astype(jnp.bfloat16)
        split[s, pl.ds(row, 16), pl.ds(0, Z)] = high
        split[s, pl.ds(row, 16), pl.ds(Z, Z)] = (value - high.astype(jnp.float32)).astype(jnp.bfloat16)

    def place_field(x, carry):
        values = []
        for s in range(S):
            for j in range(0, 4, 2):
                rows = pl.ds(8 * j, 16)
                value = raw[s, x, rows, :]
                for k in range(1, K):
                    value = jnp.where(wide_group == k, raw[orders[k][s], x, rows, :], value)
                values.append(value * scale[s])
        for s in range(S):
            for j in range(0, 4, 2):
                value = values[2 * s + j // 2]
                g0[s, x + 1, pl.ds(8 + 8 * j, 16), :] = value
                keep_split(s, pl.multiple_of(x * B, B) + 8 * j, value)
        return carry

    lax.fori_loop(0, B, place_field, 0)

    def sweep(g, i, use):
        rows = pl.ds(pl.multiple_of(i * CHUNK * B, CHUNK * B), CHUNK * B)
        depth = [
            lax.dot_general(
                split[s, rows, :], couple[s], (((1,), (0,)), ((), ())), preferred_element_type=jnp.float32
            )
            for s in range(S)
        ]
        for part in range(CHUNK):
            x = i * CHUNK + part + 1
            for j in range(4):
                row = 8 + 8 * j
                own = [g[s, x, pl.ds(row, 8), :] for s in range(S)]
                squares = own[0] * own[0]
                for s in range(1, S):
                    squares = squares + own[s] * own[s]
                sums = []
                for s in range(S):
                    total = g[s, x - 1, pl.ds(row, 8), :] + g[s, x + 1, pl.ds(row, 8), :]
                    total = total + (g[s, x, pl.ds(row - 1, 8), :] + g[s, x, pl.ds(row + 1, 8), :])
                    sums.append(total + depth[s][part * B + 8 * j : part * B + 8 * j + 8])
                use(x, j, own, squares, sums)

    def first(x, j, own, squares, sums):
        level = (1.0 - 6.0 * GRADIENT) - MIX * squares
        for s in range(S):
            change = own[s] * (level + own[s] * own[s]) + sums[s]
            g1[s, x, pl.ds(8 + 8 * j, 8), :] = own[s] + mm[s] * change

    def first_sweep(i, carry):
        sweep(g0, i, first)
        return carry

    lax.fori_loop(0, B // CHUNK, first_sweep, 0)

    own_now = code[1]
    for f in range(4):
        finish(2, f)
        for step in range(2):
            index = jnp.zeros((8, Z), jnp.int32)
            value = jnp.zeros((8, Z), jnp.float32)
            for s in range(S):
                other = jnp.broadcast_to(code_in[f, step, pl.ds(s, 1), :], (8, Z))
                same = (other == own_now) & (own_now > 0)
                index = jnp.where(same, s, index)
                value = jnp.where(same, (ROOT, 1.0)[step] * mob[...], value)
            move[step, f] = index
            weight[step, f] = value

    def add_faces(base, stride_s, stride_x, first_x, first_y, step, f):
        finish(step, f)
        flat = base.reshape(S * stride_s, Z)
        source = face_in.at[step, f].reshape(S * B, Z)
        turn, gain = move[step, f], weight[step, f]

        def eight(n, carry):
            places, values = [], []
            for i in range(8):
                cell = 8 * n + i
                got = jnp.take_along_axis(source[pl.ds(cell, 8, stride=B), :], turn, axis=0)
                if f < 2:
                    row = (first_x + (0, B - 1)[f]) * stride_x + first_y + cell
                else:
                    row = (first_x + cell) * stride_x + first_y + (0, B - 1)[f - 2]
                at = (pl.ds(row, 8, stride=stride_s), slice(None))
                places.append(at)
                values.append(flat[at] + gain * got)
            for at, value in zip(places, values):
                flat[at] = value
            return carry

        lax.fori_loop(0, B // 8, eight, 0)

    for f in range(4):
        add_faces(g1, PLANE, YP, 1, 8, 0, f)

    everyone = pltpu.make_async_remote_copy(
        send.at[pl.ds(0, nd - 1)], recv.at[pl.ds(0, nd - 1)], heat_send, heat_recv,
        device_id=(tx, ty), device_id_type=MESH,
    )
    everyone.wait_send()
    everyone.wait_recv()
    locator = jnp.broadcast_to(locator_ref[...], (Z, Z))
    order = jnp.where(locator == lax.broadcasted_iota(jnp.int32, (Z, Z), 0), 1.0, 0.0).astype(jnp.bfloat16)
    flat_recv = recv.reshape(nd * 8, Z)
    for s in range(8):
        value = (UNDERCOOL / ROOT) * (1.0 - flat_recv[pl.ds(s, nd, stride=8), :])
        value = jnp.transpose(value)
        high = value.astype(jnp.bfloat16)
        low = (value - high.astype(jnp.float32)).astype(jnp.bfloat16)
        dims = (((1,), (1,)), ((), ()))
        placed = lax.dot_general(high, order, dims, preferred_element_type=jnp.float32)
        placed = placed + lax.dot_general(low, order, dims, preferred_element_type=jnp.float32)
        for a in range(4):
            u_ref[pl.ds((8 * a + s) * B, B), :] = placed[a * B : (a + 1) * B]

    flat0, flat1 = g0.reshape(S * PLANE, Z), g1.reshape(S * PLANE, Z)

    def heat_row(side, row):
        def one(n, carry):
            u = u_ref[pl.ds(n * 8 * B + row, 8, stride=B), :]
            done = (n * 8 + sub == 0) | (n * 8 + sub == B - 1)
            u = jnp.where(done, 0.0, u)
            values = []
            for s in range(S):
                at = (pl.ds(s * PLANE + (n * 8 + 1) * YP + 8 + row, 8, stride=YP), slice(None))
                own = flat0[at]
                values.append(flat1[at] + (mm[s] * u) * (own * (ROOT - own)))
            for s in range(S):
                face_y[1, side, s, pl.ds(pl.multiple_of(n * 8, 8), 8), :] = values[s]
            return carry

        lax.fori_loop(0, B // 8, one, 0)

    def heat_term(x):
        for j in (0, 2):
            u = u_ref[pl.ds((x - 1) * B + 8 * j, 16), :]
            values = []
            for s in range(S):
                at = (s, x, pl.ds(8 + 8 * j, 16), slice(None))
                own = g0[at]
                gain = jnp.concatenate([mm[s], mm[s]], axis=0)
                values.append(g1[at] + (gain * u) * (own * (ROOT - own)))
            for s in range(S):
                g1[s, x, pl.ds(8 + 8 * j, 16), :] = values[s]
                keep_split(s, pl.multiple_of((x - 1) * B, B) + 8 * j, values[s])

    heat_term(1)
    begin(1, 0)
    heat_term(B)
    begin(1, 1)
    heat_row(0, 0)
    begin(1, 2)
    heat_row(1, B - 1)
    begin(1, 3)

    def heat_rest(x, carry):
        heat_term(x)
        return carry

    lax.fori_loop(2, B, heat_rest, 0)

    def second(x, j, own, squares, sums):
        u = u_ref[pl.ds((x - 1) * B + 8 * j, 8), :]
        level = (1.0 - 6.0 * GRADIENT) + ROOT * u - MIX * squares
        for s in range(S):
            change = own[s] * (level + own[s] * (own[s] - u)) + sums[s]
            out[s, x - 1, pl.ds(8 * j, 8), :] = own[s] + mm[s] * change

    def second_sweep(i, carry):
        sweep(g1, i, second)
        return carry

    lax.fori_loop(0, B // CHUNK, second_sweep, 0)
    for f in range(4):
        add_faces(out, B * B, B, 0, 0, 1, f)


def restore(order, moved, result_hbm, result, out_sem):
    group = lax.broadcasted_iota(jnp.int32, (8, Z), 1) // B
    places = [[order[k, s] for s in range(S)] for k in range(K)]

    def piece(i):
        planes = pl.ds(i * PIECE, PIECE)
        return pltpu.make_async_copy(result.at[:, planes], result_hbm.at[:, planes], out_sem)

    def plane(x):
        values = []
        for s in range(S):
            for j in range(4):
                rows = pl.ds(8 * j, 8)
                value = moved[s, x, rows, :]
                for k in range(1, K):
                    value = jnp.where(group == k, moved[places[k][s], x, rows, :], value)
                values.append(value * (1.0 / ROOT))
        for s in range(S):
            for j in range(4):
                result[s, x, pl.ds(8 * j, 8), :] = values[4 * s + j]

    def one(i, carry):
        for x in range(PIECE):
            plane(i * PIECE + x)
        piece(i).start()
        return carry

    lax.fori_loop(0, B // PIECE, one, 0)
    pltpu.make_async_copy(result, result_hbm, out_sem).wait()


def on_device(ntx, nty, field, heat, label, count, speed, locator):
    nd = ntx * nty
    in_hbm = pl.BlockSpec(memory_space=pltpu.HBM)
    f32, i32 = jnp.float32, jnp.int32
    moved, order = pl.pallas_call(
        functools.partial(kernel, ntx, nty),
        out_shape=(pltpu.VMEM(field.shape, f32), pltpu.SMEM((K, S), i32)),
        in_specs=[in_hbm] * 6,
        out_specs=(pl.BlockSpec(memory_space=pltpu.VMEM), pl.BlockSpec(memory_space=pltpu.SMEM)),
        scratch_shapes=[
            pltpu.VMEM((S, B, B, Z), f32),
            pltpu.VMEM((S, XP, YP, Z), f32),
            pltpu.VMEM((S, XP, YP, Z), f32),
            pltpu.VMEM(heat.shape[1:], f32),
            pltpu.VMEM((nd, 8, Z), f32),
            pltpu.VMEM((nd, 8, Z), f32),
            pltpu.VMEM((B * B, Z), f32),
            pltpu.VMEM((S, B * B, 2 * Z), jnp.bfloat16),
            pltpu.VMEM((S, 2 * Z, Z), jnp.bfloat16),
            pltpu.SMEM(label.shape, i32),
            pltpu.SMEM(count.shape, i32),
            pltpu.SMEM(speed.shape, f32),
            pltpu.VMEM((1, Z), i32),
            pltpu.VMEM((2, 8, Z), i32),
            pltpu.VMEM((4, 2, 8, Z), i32),
            pltpu.VMEM((2, 2, S, B, Z), f32),
            pltpu.VMEM((2, 4, S, B, Z), f32),
            pltpu.VMEM((2, 4, 8, Z), i32),
            pltpu.VMEM((2, 4, 8, Z), f32),
            pltpu.VMEM((8, Z), f32),
            pltpu.VMEM((S, 8, Z), f32),
            pltpu.SemaphoreType.REGULAR((nty,)),
            pltpu.SemaphoreType.DMA((6,)),
            pltpu.SemaphoreType.DMA,
            pltpu.SemaphoreType.DMA,
            pltpu.SemaphoreType.DMA((12,)),
            pltpu.SemaphoreType.DMA((12,)),
            pltpu.SemaphoreType.DMA((12,)),
        ],
        compiler_params=pltpu.CompilerParams(
            collective_id=0, has_side_effects=True, vmem_limit_bytes=59 * 2**20
        ),
        name="grains",
    )(field, heat, label, count, speed, locator.reshape(1, Z))
    return pl.pallas_call(
        restore,
        out_shape=jax.ShapeDtypeStruct(field.shape, f32),
        in_specs=[pl.BlockSpec(memory_space=pltpu.SMEM), pl.BlockSpec(memory_space=pltpu.VMEM)],
        out_specs=in_hbm,
        scratch_shapes=[
            pltpu.VMEM(field.shape, f32),
            pltpu.SemaphoreType.DMA,
        ],
        compiler_params=pltpu.CompilerParams(vmem_limit_bytes=32 * 2**20),
        name="restore",
    )(order, moved)


def solution(mesh):
    ntx, nty = mesh.shape["track"], mesh.shape["cross"]
    return jax.shard_map(
        functools.partial(on_device, ntx, nty),
        mesh=mesh,
        in_specs=(
            P(None, "track", "cross", None),
            P(("track", "cross"), None, None),
            P("track", "cross", None, None),
            P("track", "cross", None),
            P(),
            P(),
        ),
        out_specs=P(None, "track", "cross", None),
        check_vma=False,
    )
```
